128 devices in a mesh: tm: 8 (over y_lo, x), space: 16 (over y_hi, z, core).
Axes of the slice: x: 4, y: 4 (y_hi: 2, y_lo: 2; y = y_hi * 2 + y_lo), z: 4, core: 2. Of those that a mesh axis runs over, the one named last changes fastest.
Arguments:
- query_time: bfloat16 [64, 1024, 1152], P('tm', 'space'), may hold values from -6 to 6
- key_time: bfloat16 [64, 1024, 1152], P('tm', 'space'), may hold values from -6 to 6
- value_time: bfloat16 [64, 1024, 1152], P('tm', 'space'), may hold values from -6 to 6
- query_space: bfloat16 [64, 1024, 1152], P('tm', 'space'), may hold values from -6 to 6
- key_space: bfloat16 [64, 1024, 1152], P('tm', 'space'), may hold values from -6 to 6
- value_space: bfloat16 [64, 1024, 1152], P('tm', 'space'), may hold values from -6 to 6
- grad_output: bfloat16 [64, 1024, 1152], P('tm', 'space'), may hold values from -6 to 6
- outproj_time: bfloat16 [1152, 1152], replicated, may hold values from -0.1875 to 0.1875
- queryproj_time: bfloat16 [1152, 1152], replicated, may hold values from -0.1875 to 0.1875
- keyproj_time: bfloat16 [1152, 1152], replicated, may hold values from -0.1875 to 0.1875
- valueproj_time: bfloat16 [1152, 1152], replicated, may hold values from -0.1875 to 0.1875
- outproj_space: bfloat16 [1152, 1152], replicated, may hold values from -0.1875 to 0.1875
Outputs:
- query_grad: bfloat16 [64, 1024, 1152], P('tm', 'space')
- key_grad: bfloat16 [64, 1024, 1152], P('tm', 'space')
- value_grad: bfloat16 [64, 1024, 1152], P('tm', 'space')
- middle_grad: bfloat16 [64, 1024, 1152], P('tm', 'space')
The draws below stay inside these ranges and needn't reach their ends.
All inputs are finite; a program needn't handle non-finite values.
Results may differ from the reference program's by a relative error of at most 0.03.
Values may be sent and summed in bfloat16 or wider, within the bound.
No kernel may reach another device: no remote copies, remote signals or barrier semaphores. Data moves between devices by JAX's collectives and lax.ppermute only.
A program may use at most 128 MiB of HBM per device.

```python
import jax
import jax.numpy as jnp
from jax import lax

HEAD_DIM = 72
D = 1152
PA_DEV = 64
FRAMES = 64
PATCHES = 1024
N_SPACE = 16


def drawn_bulk(key):
    return jnp.clip(jax.random.normal(key, (FRAMES, PATCHES, D), jnp.float32), -6.0, 6.0)


def draw_query_time(key, part):
    key = jax.random.fold_in(key, 3)
    return drawn_bulk(key).astype(jnp.bfloat16)


def draw_key_time(key, part):
    key = jax.random.fold_in(key, 5)
    return drawn_bulk(key).astype(jnp.bfloat16)


def draw_query_space(key, part):
    key = jax.random.fold_in(key, 7)
    return drawn_bulk(key).astype(jnp.bfloat16)


def draw_key_space(key, part):
    key = jax.random.fold_in(key, 9)
    return drawn_bulk(key).astype(jnp.bfloat16)


def levels(rng, shape, shards, low, top_value):
    def one(dim, parts):
        heights = jax.random.uniform(jax.random.fold_in(jax.random.fold_in(rng, 6), dim), (parts,), jnp.float32, low / len(shards), top_value / len(shards))
        return jnp.repeat(jnp.exp(heights), shape[dim] // parts).reshape((-1,) + (1,) * (len(shape) - dim - 1))

    loudness = one(*shards[0])
    for cut in shards[1:]:
        loudness = loudness * one(*cut)
    return loudness


def normal_values(stream_key, dims, scale, limit, split=(), dtype=jnp.bfloat16):
    entries = scale * jax.random.normal(stream_key, dims, jnp.float32)
    if split:
        entries = entries * levels(stream_key, dims, split, -0.22, 0.18)
    return jnp.clip(entries, -limit, limit).astype(dtype)


def setup_inputs(seed: int = 0) -> dict:
    seeds = jax.random.split(jax.random.key(seed), 13)
    query_time = draw_query_time(jax.random.fold_in(seeds[12], 71), 0)
    key_time = draw_key_time(jax.random.fold_in(seeds[12], 71), 0)
    value_time = normal_values(seeds[2], (FRAMES, PATCHES, D), 1.0, 6.0, ((0, 8), (1, 16)))
    query_space = draw_query_space(jax.random.fold_in(seeds[12], 71), 0)
    key_space = draw_key_space(jax.random.fold_in(seeds[12], 71), 0)
    value_space = normal_values(seeds[5], (FRAMES, PATCHES, D), 1.0, 6.0, ((0, 8), (1, 16)))
    grad_output = normal_values(seeds[6], (FRAMES, PATCHES, D), 1.0, 6.0, ((0, 8), (1, 16)))
    outproj_time = normal_values(seeds[7], (D, D), D ** -0.5, 0.1875)
    queryproj_time = normal_values(seeds[8], (D, D), D ** -0.5, 0.1875)
    keyproj_time = normal_values(seeds[9], (D, D), D ** -0.5, 0.1875)
    valueproj_time = normal_values(seeds[10], (D, D), D ** -0.5, 0.1875)
    outproj_space = normal_values(seeds[11], (D, D), D ** -0.5, 0.1875)
    return {"query_time": query_time, "key_time": key_time, "value_time": value_time, "query_space": query_space, "key_space": key_space, "value_space": value_space, "grad_output": grad_output, "outproj_time": outproj_time, "queryproj_time": queryproj_time, "keyproj_time": keyproj_time, "valueproj_time": valueproj_time, "outproj_space": outproj_space}


def back_project(rows, weight):
    flat = rows.reshape(-1, rows.shape[-1])
    result = jnp.dot(flat, weight.T, preferred_element_type=jnp.float32)
    return result.reshape(rows.shape[:-1] + (weight.shape[0],))


def attend_back(query, keys, values, grad, layout):
    query, keys, values, grad = lax.optimization_barrier((query, keys, values, grad))
    leading = query.shape[:-1]
    head_count = query.shape[-1] // HEAD_DIM
    query, keys, values, grad = [member.reshape(leading + (head_count, HEAD_DIM)).astype(jnp.float32) for member in (query, keys, values, grad)]
    partner = layout.replace("l", "m")
    factor = HEAD_DIM ** -0.5
    scores = jnp.einsum(layout + "," + partner + "->bhlm", query, keys) * factor
    weights = jax.nn.softmax(scores, axis=-1)
    weights_half = lax.optimization_barrier(weights.astype(jnp.bfloat16)).astype(jnp.float32)
    grad_weights = jnp.einsum(layout + "," + partner + "->bhlm", grad, values)
    centre = jnp.sum(weights * grad_weights, axis=-1, keepdims=True)
    grad_scores = lax.optimization_barrier((weights * (grad_weights - centre)).astype(jnp.bfloat16)).astype(jnp.float32)
    query_grad = (jnp.einsum("bhlm," + partner + "->" + layout, grad_scores, keys) * factor).astype(jnp.bfloat16)
    key_grad = (jnp.einsum("bhlm," + layout + "->" + partner, grad_scores, query) * factor).astype(jnp.bfloat16)
    value_grad = jnp.einsum("bhlm," + layout + "->" + partner, weights_half, grad).astype(jnp.bfloat16)
    return tuple(member.reshape(leading + (head_count * HEAD_DIM,)) for member in (query_grad, key_grad, value_grad))


def reference(query_time, key_time, value_time, query_space, key_space, value_space, grad_output, outproj_time, queryproj_time, keyproj_time, valueproj_time, outproj_space):
    grad_time = back_project(grad_output, outproj_time).astype(jnp.bfloat16)

    def blocks(array):
        return array.reshape(FRAMES, N_SPACE, PA_DEV, D).transpose(1, 0, 2, 3)

    def unblock(array):
        return array.transpose(1, 0, 2, 3).reshape(FRAMES, PATCHES, D)

    def time_block(members):
        return attend_back(members[0], members[1], members[2], members[3], "lbhe")

    time_grads = lax.map(time_block, (blocks(query_time), blocks(key_time), blocks(value_time), blocks(grad_time)))
    grad_qt, grad_kt, grad_vt = [unblock(member) for member in time_grads]
    middle = grad_output.astype(jnp.float32) + back_project(grad_qt, queryproj_time) + back_project(grad_kt, keyproj_time) + back_project(grad_vt, valueproj_time)
    middle_grad = middle.astype(jnp.bfloat16)
    grad_space = back_project(middle_grad, outproj_space).astype(jnp.bfloat16)

    def one_frame(members):
        expanded = [member[None] for member in members]
        result = attend_back(expanded[0], expanded[1], expanded[2], expanded[3], "blhe")
        return tuple(member[0] for member in result)

    query_grad, key_grad, value_grad = lax.map(one_frame, (query_space, key_space, value_space, grad_space))
    return query_grad, key_grad, value_grad, middle_grad
```

```python
import jax
import jax.numpy as jnp
from jax import lax
from jax.experimental import pallas as pl
from jax.experimental.pallas import tpu as pltpu
from jax.sharding import PartitionSpec as P

HEAD_DIM = 72
D = 1152
HALF = 640
SCALE = HEAD_DIM**-0.5
LOG2E = 1.4426950408889634
BF = jnp.bfloat16
F32 = jnp.float32
VMEM_LIMIT = 56 * 1024 * 1024


def nn(a, b):
    return lax.dot_general(a, b, (((1,), (0,)), ((), ())), preferred_element_type=F32)


def nt(a, b):
    return lax.dot_general(a, b, (((1,), (1,)), ((), ())), preferred_element_type=F32)


def tn(a, b):
    return lax.dot_general(a, b, (((0,), (0,)), ((), ())), preferred_element_type=F32)


def lane_mask(rows, low):
    lane = lax.broadcasted_iota(jnp.int32, (rows, 256), 1)
    return (lane >= low) & (lane < low + HEAD_DIM)


def permutation(inner):
    outer = 512 // inner
    row = lax.broadcasted_iota(jnp.int32, (512, 512), 0)
    column = lax.broadcasted_iota(jnp.int32, (512, 512), 1)
    return (column == inner * (row % outer) + row // outer).astype(BF)


def temporal_kernel(
    r_ref, wo_hbm, wq_hbm, wk_hbm, wv_hbm, out_ref,
    wo, wq, wk, wv, q, k, v, g0, g, dq, dk, dv, sems,
):
    copies = [
        pltpu.make_async_copy(src, dst, sems.at[i])
        for i, (src, dst) in enumerate(((wo_hbm, wo), (wq_hbm, wq), (wk_hbm, wk), (wv_hbm, wv)))
    ]
    for copy in copies:
        copy.start()
    to_patch = permutation(8)
    for a, dst in enumerate((q, k, v, g0)):
        dst[...] = nn(to_patch, r_ref[:, a].reshape(512, D)).astype(BF)
    copies[0].wait()
    g[...] = nt(g0[...], wo[...]).astype(BF)
    m_patch = lax.broadcasted_iota(jnp.int32, (128, 128), 0) // 64
    l_patch = lax.broadcasted_iota(jnp.int32, (128, 128), 1) // 64
    same = m_patch == l_patch

    def head(h, carry):
        first = jnp.minimum(h * HEAD_DIM // 128, D // 128 - 2) * 128
        window = pl.ds(pl.multiple_of(first, 128), 256)
        mask = lane_mask(128, h * HEAD_DIM - first)
        for b in range(4):
            rows = pl.ds(b * 128, 128)
            qb, kb, vb, gb = [ref[rows, window] for ref in (q, k, v, g)]
            kh = jnp.where(mask, kb, jnp.zeros_like(kb))
            vh = jnp.where(mask, vb, jnp.zeros_like(vb))
            s = jnp.where(same, nt(kh, qb) * (SCALE * LOG2E), -1e30)
            p = jnp.exp2(s - jnp.max(s, axis=0, keepdims=True))
            p = p * (1.0 / jnp.sum(p, axis=0, keepdims=True))
            dp = nt(vh, gb)
            delta = jnp.sum(p * dp, axis=0, keepdims=True)
            ds = (p * (dp - delta)).astype(BF)
            new_dk = (nn(ds, qb) * SCALE).astype(BF)
            new_dv = nn(p.astype(BF), gb).astype(BF)
            new_dq = (tn(ds, kb) * SCALE).astype(BF)
            for ref, new in ((dq, new_dq), (dk, new_dk), (dv, new_dv)):
                ref[rows, window] = jnp.where(mask, new, ref[rows, window])
        return carry

    lax.fori_loop(0, D // HEAD_DIM, head, 0)
    for copy in copies[1:]:
        copy.wait()
    middle = (
        g0[...].astype(F32)
        + nt(dq[...], wq[...])
        + nt(dk[...], wk[...])
        + nt(dv[...], wv[...])
    ).astype(BF)
    out_ref[...] = nn(permutation(64), middle).astype(BF).reshape(8, 64, D)


def temporal(r, wo, wq, wk, wv):
    hbm = pl.BlockSpec(memory_space=pl.ANY)
    vmem = pl.BlockSpec(memory_space=pltpu.VMEM)
    weight = pltpu.VMEM((D, D), BF)
    rows = pltpu.VMEM((512, D), BF)
    return pl.pallas_call(
        temporal_kernel,
        out_shape=jax.ShapeDtypeStruct((8, 64, D), BF),
        in_specs=[vmem, hbm, hbm, hbm, hbm],
        out_specs=vmem,
        scratch_shapes=[weight] * 4 + [rows] * 8 + [pltpu.SemaphoreType.DMA((4,))],
        compiler_params=pltpu.CompilerParams(vmem_limit_bytes=VMEM_LIMIT),
        cost_estimate=pl.CostEstimate(
            flops=20_000_000_000, bytes_accessed=16_000_000, transcendentals=2_000_000
        ),
        name="temporal",
    )(r, wo, wq, wk, wv)


def project_kernel(m_ref, w_ref, middle_ref, gs_ref):
    row = lax.broadcasted_iota(jnp.int32, (512, 512), 0)
    column = lax.broadcasted_iota(jnp.int32, (512, 512), 1)
    frame, block, low = row // 64, (row // 8) % 8, row % 8
    perm = (column == block * 64 + frame * 8 + low).astype(BF)
    middle = nn(perm, m_ref[...].reshape(512, D)).astype(BF)
    middle_ref[...] = middle.reshape(8, 64, D)
    gs = nt(middle, w_ref[...]).astype(BF).reshape(8, 64, D)
    gs_ref[:, 0] = gs[:, :, :HALF]
    gs_ref[:, 1] = gs[:, :, D - HALF :]


def project(m, w):
    vmem = pl.BlockSpec(memory_space=pltpu.VMEM)
    return pl.pallas_call(
        project_kernel,
        out_shape=(
            jax.ShapeDtypeStruct((8, 64, D), BF),
            jax.ShapeDtypeStruct((8, 2, 64, HALF), BF),
        ),
        in_specs=[vmem, vmem],
        out_specs=(vmem, vmem),
        compiler_params=pltpu.CompilerParams(vmem_limit_bytes=VMEM_LIMIT),
        cost_estimate=pl.CostEstimate(
            flops=4_000_000_000, bytes_accessed=8_000_000, transcendentals=0
        ),
        name="project",
    )(m, w)


def spatial_kernel(base_ref, qkv_ref, g_ref, out_ref, qh, kh, vh, gh, dk, dv):
    base = base_ref[0]

    def head(j, carry):
        first = (j // 2) * 128
        window = pl.ds(pl.multiple_of(first, 128), 256)
        mask = lane_mask(1024, base + j * HEAD_DIM - first)
        for dst, src in (
            (qh, qkv_ref[:, 0, :, window]),
            (kh, qkv_ref[:, 1, :, window]),
            (vh, qkv_ref[:, 2, :, window]),
            (gh, g_ref[:, :, window]),
        ):
            src = src.reshape(1024, 256)
            dst[...] = jnp.where(mask, src, jnp.zeros_like(src))
        dk[...] = jnp.zeros_like(dk)
        dv[...] = jnp.zeros_like(dv)

        def block(i, inner):
            rows = pl.ds(pl.multiple_of(i * 256, 256), 256)
            qb, gb = qh[rows], gh[rows]
            s = nt(kh[...], qb) * (SCALE * LOG2E)
            p = jnp.exp2(s - jnp.max(s, axis=0, keepdims=True))
            p = p * (1.0 / jnp.sum(p, axis=0, keepdims=True))
            dp = nt(vh[...], gb)
            delta = jnp.sum(p * dp, axis=0, keepdims=True)
            ds = (p * (dp - delta)).astype(BF)
            dk[...] += nn(ds, qb)
            dv[...] += nn(p.astype(BF), gb)
            new_dq = (tn(ds, kh[...]) * SCALE).astype(BF).reshape(4, 64, 256)
            four = pl.ds(i * 4, 4)
            out_ref[four, 0, :, window] = jnp.where(
                mask[:256].reshape(4, 64, 256), new_dq, out_ref[four, 0, :, window]
            )
            return inner

        lax.fori_loop(0, 4, block, 0)
        deep = mask.reshape(16, 64, 256)
        for a, new in ((1, dk[...] * SCALE), (2, dv[...])):
            out_ref[:, a, :, window] = jnp.where(
                deep, new.astype(BF).reshape(16, 64, 256), out_ref[:, a, :, window]
            )
        return carry

    lax.fori_loop(0, 8, head, 0)


def spatial(base, qkv, g):
    vmem = pl.BlockSpec(memory_space=pltpu.VMEM)
    return pl.pallas_call(
        spatial_kernel,
        out_shape=jax.ShapeDtypeStruct((16, 3, 64, HALF), BF),
        in_specs=[pl.BlockSpec(memory_space=pltpu.SMEM), vmem, vmem],
        out_specs=vmem,
        scratch_shapes=[pltpu.VMEM((1024, 256), BF)] * 4 + [pltpu.VMEM((1024, 256), F32)] * 2,
        compiler_params=pltpu.CompilerParams(vmem_limit_bytes=VMEM_LIMIT),
        cost_estimate=pl.CostEstimate(
            flops=22_000_000_000, bytes_accessed=9_000_000, transcendentals=8_400_000
        ),
        name="spatial",
    )(base, qkv, g)


def unpack_kernel(r_ref, *out_refs):
    lane = lax.broadcasted_iota(jnp.int32, (64, 128), 1)
    for a, out in enumerate(out_refs):
        out[0, :, :512] = r_ref[0, 0, a, :, :512]
        out[0, :, 512:640] = jnp.where(
            lane < 64, r_ref[0, 0, a, :, 512:640], r_ref[0, 1, a, :, :128]
        )
        out[0, :, 640:] = r_ref[0, 1, a, :, 128:]


def unpack(r):
    whole = jax.ShapeDtypeStruct((8, 64, D), BF)
    return pl.pallas_call(
        unpack_kernel,
        out_shape=(whole,) * 3,
        grid=(8,),
        in_specs=[pl.BlockSpec((1, 2, 3, 64, HALF), lambda f: (f, 0, 0, 0, 0))],
        out_specs=(pl.BlockSpec((1, 64, D), lambda f: (f, 0, 0)),) * 3,
        compiler_params=pltpu.CompilerParams(vmem_limit_bytes=VMEM_LIMIT),
        name="unpack",
    )(r)


def exchange(x, axis):
    return lax.all_to_all(x, axis, 0, 0, tiled=True)


def per_device(
    query_time, key_time, value_time, query_space, key_space, value_space, grad_output,
    outproj_time, queryproj_time, keyproj_time, valueproj_time, outproj_space,
):
    t = jnp.stack([query_time, key_time, value_time, grad_output])
    t = t.reshape(4, 8, 8, 8, D).transpose(2, 0, 1, 3, 4).reshape(8, 4, 64, D)
    t = exchange(t, "tm")
    middle = temporal(t, outproj_time, queryproj_time, keyproj_time, valueproj_time)
    middle = exchange(middle, "tm")
    middle_grad, gs = project(middle, outproj_space)
    s = jnp.stack([query_space, key_space, value_space], axis=1)
    s = jnp.stack([s[..., :HALF], s[..., D - HALF :]], axis=1).reshape(16, 3, 64, HALF)
    s = exchange(s, "space")
    gs = exchange(gs.reshape(16, 64, HALF), "space")
    base = (lax.axis_index("space") % 2 * 64).astype(jnp.int32).reshape(1)
    out = exchange(spatial(base, s, gs), "space")
    query_grad, key_grad, value_grad = unpack(out.reshape(8, 2, 3, 64, HALF))
    return query_grad, key_grad, value_grad, middle_grad


def solution(mesh):
    bulk = P("tm", "space", None)
    return jax.shard_map(
        per_device,
        mesh=mesh,
        in_specs=(bulk,) * 7 + (P(),) * 5,
        out_specs=(bulk,) * 4,
        check_vma=False,
    )
```

```python
import jax
import jax.numpy as jnp
from jax import lax
from jax.experimental import pallas as pl
from jax.experimental.pallas import tpu as pltpu
from jax.sharding import PartitionSpec as P

HEAD_DIM = 72
D = 1152
HALF = 640
SCALE = HEAD_DIM**-0.5
LOG2E = 1.4426950408889634
BF = jnp.bfloat16
F32 = jnp.float32
VMEM_LIMIT = 56 * 1024 * 1024


def nn(a, b):
    return lax.dot_general(a, b, (((1,), (0,)), ((), ())), preferred_element_type=F32)


def nt(a, b):
    return lax.dot_general(a, b, (((1,), (1,)), ((), ())), preferred_element_type=F32)


def tn(a, b):
    return lax.dot_general(a, b, (((0,), (0,)), ((), ())), preferred_element_type=F32)


def lane_mask(rows, low):
    lane = lax.broadcasted_iota(jnp.int32, (rows, 256), 1)
    return (lane >= low) & (lane < low + HEAD_DIM)


def permutation(inner):
    outer = 512 // inner
    row = lax.broadcasted_iota(jnp.int32, (512, 512), 0)
    column = lax.broadcasted_iota(jnp.int32, (512, 512), 1)
    return (column == inner * (row % outer) + row // outer).astype(BF)


def temporal_kernel(
    r_ref, wo_hbm, wq_hbm, wk_hbm, wv_hbm, out_ref,
    wo, wq, wk, wv, q, k, v, g0, g, dq, dk, dv, sems,
):
    copies = [
        pltpu.make_async_copy(src, dst, sems.at[i])
        for i, (src, dst) in enumerate(((wo_hbm, wo), (wq_hbm, wq), (wk_hbm, wk), (wv_hbm, wv)))
    ]
    for copy in copies:
        copy.start()
    to_patch = permutation(8)
    for a, dst in enumerate((q, k, v, g0)):
        dst[...] = nn(to_patch, r_ref[:, a].reshape(512, D)).astype(BF)
    copies[0].wait()
    g[...] = nt(g0[...], wo[...]).astype(BF)
    m_patch = lax.broadcasted_iota(jnp.int32, (128, 128), 0) // 64
    l_patch = lax.broadcasted_iota(jnp.int32, (128, 128), 1) // 64
    same = m_patch == l_patch

    def head(h, carry):
        first = jnp.minimum(h * HEAD_DIM // 128, D // 128 - 2) * 128
        window = pl.ds(pl.multiple_of(first, 128), 256)
        mask = lane_mask(128, h * HEAD_DIM - first)
        for b in range(4):
            rows = pl.ds(b * 128, 128)
            qb, kb, vb, gb = [ref[rows, window] for ref in (q, k, v, g)]
            kh = jnp.where(mask, kb, jnp.zeros_like(kb))
            vh = jnp.where(mask, vb, jnp.zeros_like(vb))
            s = jnp.where(same, nt(kh, qb) * (SCALE * LOG2E), -1e30)
            p = jnp.exp2(s - jnp.max(s, axis=0, keepdims=True))
            p = p * (1.0 / jnp.sum(p, axis=0, keepdims=True))
            dp = nt(vh, gb)
            delta = jnp.sum(p * dp, axis=0, keepdims=True)
            ds = (p * (dp - delta)).astype(BF)
            new_dk = (nn(ds, qb) * SCALE).astype(BF)
            new_dv = nn(p.astype(BF), gb).astype(BF)
            new_dq = (tn(ds, kb) * SCALE).astype(BF)
            for ref, new in ((dq, new_dq), (dk, new_dk), (dv, new_dv)):
                ref[rows, window] = jnp.where(mask, new, ref[rows, window])
        return carry

    lax.fori_loop(0, D // HEAD_DIM, head, 0)
    for copy in copies[1:]:
        copy.wait()
    middle = (
        g0[...].astype(F32)
        + nt(dq[...], wq[...])
        + nt(dk[...], wk[...])
        + nt(dv[...], wv[...])
    ).astype(BF)
    out_ref[...] = nn(permutation(64), middle).astype(BF).reshape(8, 64, D)


def temporal(r, wo, wq, wk, wv):
    hbm = pl.BlockSpec(memory_space=pl.ANY)
    vmem = pl.BlockSpec(memory_space=pltpu.VMEM)
    weight = pltpu.VMEM((D, D), BF)
    rows = pltpu.VMEM((512, D), BF)
    return pl.pallas_call(
        temporal_kernel,
        out_shape=jax.ShapeDtypeStruct((8, 64, D), BF),
        in_specs=[vmem, hbm, hbm, hbm, hbm],
        out_specs=vmem,
        scratch_shapes=[weight] * 4 + [rows] * 8 + [pltpu.SemaphoreType.DMA((4,))],
        compiler_params=pltpu.CompilerParams(vmem_limit_bytes=VMEM_LIMIT),
        cost_estimate=pl.CostEstimate(
            flops=20_000_000_000, bytes_accessed=16_000_000, transcendentals=2_000_000
        ),
        name="temporal",
    )(r, wo, wq, wk, wv)


def project_kernel(m_ref, w_ref, v_ref, middle_ref, vg_ref):
    row = lax.broadcasted_iota(jnp.int32, (512, 512), 0)
    column = lax.broadcasted_iota(jnp.int32, (512, 512), 1)
    frame, block, low = row // 64, (row // 8) % 8, row % 8
    perm = (column == block * 64 + frame * 8 + low).astype(BF)
    middle = nn(perm, m_ref[...].reshape(512, D)).astype(BF)
    middle_ref[...] = middle.reshape(8, 64, D)
    gs = nt(middle, w_ref[...]).astype(BF).reshape(8, 64, D)
    for half, lanes in enumerate((slice(0, HALF), slice(D - HALF, D))):
        vg_ref[:, half, 0] = v_ref[:, :, lanes]
        vg_ref[:, half, 1] = gs[:, :, lanes]


def project(m, w, v):
    vmem = pl.BlockSpec(memory_space=pltpu.VMEM)
    return pl.pallas_call(
        project_kernel,
        out_shape=(
            jax.ShapeDtypeStruct((8, 64, D), BF),
            jax.ShapeDtypeStruct((8, 2, 2, 64, HALF), BF),
        ),
        in_specs=[vmem, vmem, vmem],
        out_specs=(vmem, vmem),
        compiler_params=pltpu.CompilerParams(vmem_limit_bytes=VMEM_LIMIT),
        cost_estimate=pl.CostEstimate(
            flops=4_000_000_000, bytes_accessed=8_000_000, transcendentals=0
        ),
        name="project",
    )(m, w, v)


def head_window(j, base):
    first = (j // 2) * 128
    return pl.ds(pl.multiple_of(first, 128), 256), base + j * HEAD_DIM - first


def masked(ref, a, window, mask):
    x = ref[:, a, :, window].reshape(1024, 256)
    return jnp.where(mask, x, jnp.zeros_like(x))


def probs_kernel(base_ref, qk_ref, p_ref, kh):
    window, low = head_window(pl.program_id(0), base_ref[0])
    kh[...] = masked(qk_ref, 1, window, lane_mask(1024, low))
    for i in range(4):
        rows = slice(i * 256, (i + 1) * 256)
        qb = qk_ref[4 * i : 4 * i + 4, 0, :, window].reshape(256, 256)
        s = nt(kh[...], qb) * (SCALE * LOG2E)
        p = jnp.exp2(s - jnp.max(s, axis=0, keepdims=True))
        p_ref[0, :, rows] = (p * (1.0 / jnp.sum(p, axis=0, keepdims=True))).astype(BF)


def probs(base, qk):
    return pl.pallas_call(
        probs_kernel,
        out_shape=jax.ShapeDtypeStruct((8, 1024, 1024), BF),
        grid=(8,),
        in_specs=[
            pl.BlockSpec(memory_space=pltpu.SMEM),
            pl.BlockSpec((16, 2, 64, HALF), lambda j: (0, 0, 0, 0)),
        ],
        out_specs=pl.BlockSpec((1, 1024, 1024), lambda j: (j, 0, 0)),
        scratch_shapes=[pltpu.VMEM((1024, 256), BF)],
        compiler_params=pltpu.CompilerParams(vmem_limit_bytes=VMEM_LIMIT),
        cost_estimate=pl.CostEstimate(
            flops=20_000_000_000, bytes_accessed=20_000_000, transcendentals=8_400_000
        ),
        name="probs",
    )(base, qk)


def grads_kernel(base_ref, qk_ref, vg_ref, p_ref, out_ref, qh, kh, vh, gh, ds):
    window, low = head_window(pl.program_id(0), base_ref[0])
    mask = lane_mask(1024, low)
    for dst, ref, a in ((qh, qk_ref, 0), (kh, qk_ref, 1), (vh, vg_ref, 0), (gh, vg_ref, 1)):
        dst[...] = masked(ref, a, window, mask)
    deep = mask.reshape(16, 64, 256)

    def put(a, new):
        new = new.astype(BF).reshape(16, 64, 256)
        out_ref[:, a, :, window] = jnp.where(deep, new, out_ref[:, a, :, window])

    for i in range(4):
        rows = slice(i * 256, (i + 1) * 256)
        dp = nt(vh[...], gh[rows])
        p = p_ref[0, :, rows].astype(F32)
        delta = jnp.sum(p * dp, axis=0, keepdims=True)
        ds[:, rows] = (p * (dp - delta)).astype(BF)
    put(2, nn(p_ref[0], gh[...]))
    put(1, nn(ds[...], qh[...]) * SCALE)
    put(0, tn(ds[...], kh[...]) * SCALE)


def grads(base, qk, vg, p):
    whole = pl.BlockSpec((16, 2, 64, HALF), lambda j: (0, 0, 0, 0))
    return pl.pallas_call(
        grads_kernel,
        out_shape=jax.ShapeDtypeStruct((16, 3, 64, HALF), BF),
        grid=(8,),
        in_specs=[
            pl.BlockSpec(memory_space=pltpu.SMEM),
            whole,
            whole,
            pl.BlockSpec((1, 1024, 1024), lambda j: (j, 0, 0)),
        ],
        out_specs=pl.BlockSpec((16, 3, 64, HALF), lambda j: (0, 0, 0, 0)),
        scratch_shapes=[pltpu.VMEM((1024, 256), BF)] * 4 + [pltpu.VMEM((1024, 1024), BF)],
        compiler_params=pltpu.CompilerParams(vmem_limit_bytes=VMEM_LIMIT),
        cost_estimate=pl.CostEstimate(
            flops=22_000_000_000, bytes_accessed=26_000_000, transcendentals=0
        ),
        name="grads",
    )(base, qk, vg, p)


def unpack_kernel(r_ref, *out_refs):
    lane = lax.broadcasted_iota(jnp.int32, (8, 64, 128), 2)
    for a, out in enumerate(out_refs):
        out[:, :, :512] = r_ref[:, 0, a, :, :512]
        out[:, :, 512:640] = jnp.where(
            lane < 64, r_ref[:, 0, a, :, 512:640], r_ref[:, 1, a, :, :128]
        )
        out[:, :, 640:] = r_ref[:, 1, a, :, 128:]


def unpack(r):
    whole = jax.ShapeDtypeStruct((8, 64, D), BF)
    vmem = pl.BlockSpec(memory_space=pltpu.VMEM)
    return pl.pallas_call(
        unpack_kernel,
        out_shape=(whole,) * 3,
        in_specs=[vmem],
        out_specs=(vmem,) * 3,
        compiler_params=pltpu.CompilerParams(vmem_limit_bytes=32 * 1024 * 1024),
        name="unpack",
    )(r)


def exchange(x, axis):
    return lax.all_to_all(x, axis, 0, 0, tiled=True)


def per_device(
    query_time, key_time, value_time, query_space, key_space, value_space, grad_output,
    outproj_time, queryproj_time, keyproj_time, valueproj_time, outproj_space,
):
    base = (lax.axis_index("space") % 2 * 64).astype(jnp.int32).reshape(1)
    t = jnp.stack([query_time, key_time, value_time, grad_output])
    t = t.reshape(4, 8, 8, 8, D).transpose(2, 0, 1, 3, 4).reshape(8, 4, 64, D)
    t = exchange(t, "tm")
    qk = jnp.stack([query_space, key_space], axis=1)
    qk = jnp.stack([qk[..., :HALF], qk[..., D - HALF :]], axis=1).reshape(16, 2, 64, HALF)
    qk, t = lax.optimization_barrier((qk, t))
    qk = exchange(qk, "space")
    middle = temporal(t, outproj_time, queryproj_time, keyproj_time, valueproj_time)
    middle, qk = lax.optimization_barrier((middle, qk))
    middle = exchange(middle, "tm")
    middle_grad, vg = project(middle, outproj_space, value_space)
    vg, qk = lax.optimization_barrier((vg, qk))
    p = probs(base, qk)
    vg = exchange(vg.reshape(16, 2, 64, HALF), "space")
    out = exchange(grads(base, qk, vg, p), "space")
    query_grad, key_grad, value_grad = unpack(out.reshape(8, 2, 3, 64, HALF))
    return query_grad, key_grad, value_grad, middle_grad


def solution(mesh):
    bulk = P("tm", "space", None)
    return jax.shard_map(
        per_device,
        mesh=mesh,
        in_specs=(bulk,) * 7 + (P(),) * 5,
        out_specs=(bulk,) * 4,
        check_vma=False,
    )
```

```python
import jax
import jax.numpy as jnp
from jax import lax
from jax.experimental import pallas as pl
from jax.experimental.pallas import tpu as pltpu
from jax.sharding import PartitionSpec as P

HEAD_DIM = 72
D = 1152
ROWS = 288
SCALE = HEAD_DIM**-0.5
LOG2E = 1.4426950408889634
BF = jnp.bfloat16
F32 = jnp.float32
VMEM_LIMIT = 56 * 1024 * 1024


def nn(a, b):
    return lax.dot_general(a, b, (((1,), (0,)), ((), ())), preferred_element_type=F32)


def nt(a, b):
    return lax.dot_general(a, b, (((1,), (1,)), ((), ())), preferred_element_type=F32)


def tn(a, b):
    return lax.dot_general(a, b, (((0,), (0,)), ((), ())), preferred_element_type=F32)


def lane_mask(rows, low):
    lane = lax.broadcasted_iota(jnp.int32, (rows, 256), 1)
    return (lane >= low) & (lane < low + HEAD_DIM)


def permutation(inner):
    outer = 512 // inner
    row = lax.broadcasted_iota(jnp.int32, (512, 512), 0)
    column = lax.broadcasted_iota(jnp.int32, (512, 512), 1)
    return (column == inner * (row % outer) + row // outer).astype(BF)


def temporal_kernel(
    r_ref, wo_hbm, wq_hbm, wk_hbm, wv_hbm, out_ref,
    wo, wq, wk, wv, q, k, v, g0, g, dq, dk, dv, sems,
):
    copies = [
        pltpu.make_async_copy(src, dst, sems.at[i])
        for i, (src, dst) in enumerate(((wo_hbm, wo), (wq_hbm, wq), (wk_hbm, wk), (wv_hbm, wv)))
    ]
    for copy in copies:
        copy.start()
    to_patch = permutation(8)
    for a, dst in enumerate((q, k, v, g0)):
        dst[...] = nn(to_patch, r_ref[:, a].reshape(512, D)).astype(BF)
    copies[0].wait()
    g[...] = nt(g0[...], wo[...]).astype(BF)
    m_patch = lax.broadcasted_iota(jnp.int32, (128, 128), 0) // 64
    l_patch = lax.broadcasted_iota(jnp.int32, (128, 128), 1) // 64
    same = m_patch == l_patch

    def head(h, carry):
        first = jnp.minimum(h * HEAD_DIM // 128, D // 128 - 2) * 128
        window = pl.ds(pl.multiple_of(first, 128), 256)
        mask = lane_mask(128, h * HEAD_DIM - first)
        for b in range(4):
            rows = pl.ds(b * 128, 128)
            qb, kb, vb, gb = [ref[rows, window] for ref in (q, k, v, g)]
            kh = jnp.where(mask, kb, jnp.zeros_like(kb))
            vh = jnp.where(mask, vb, jnp.zeros_like(vb))
            s = jnp.where(same, nt(kh, qb) * (SCALE * LOG2E), -1e30)
            p = jnp.exp2(s - jnp.max(s, axis=0, keepdims=True))
            p = p * (1.0 / jnp.sum(p, axis=0, keepdims=True))
            dp = nt(vh, gb)
            delta = jnp.sum(p * dp, axis=0, keepdims=True)
            ds = (p * (dp - delta)).astype(BF)
            new_dk = (nn(ds, qb) * SCALE).astype(BF)
            new_dv = nn(p.astype(BF), gb).astype(BF)
            new_dq = (tn(ds, kb) * SCALE).astype(BF)
            for ref, new in ((dq, new_dq), (dk, new_dk), (dv, new_dv)):
                ref[rows, window] = jnp.where(mask, new, ref[rows, window])
        return carry

    lax.fori_loop(0, D // HEAD_DIM, head, 0)
    for copy in copies[1:]:
        copy.wait()
    middle = (
        g0[...].astype(F32)
        + nt(dq[...], wq[...])
        + nt(dk[...], wk[...])
        + nt(dv[...], wv[...])
    ).astype(BF)
    out_ref[...] = nn(permutation(64), middle).astype(BF).reshape(8, 64, D)


def temporal(r, wo, wq, wk, wv):
    hbm = pl.BlockSpec(memory_space=pl.ANY)
    vmem = pl.BlockSpec(memory_space=pltpu.VMEM)
    weight = pltpu.VMEM((D, D), BF)
    rows = pltpu.VMEM((512, D), BF)
    return pl.pallas_call(
        temporal_kernel,
        out_shape=jax.ShapeDtypeStruct((8, 64, D), BF),
        in_specs=[vmem, hbm, hbm, hbm, hbm],
        out_specs=vmem,
        scratch_shapes=[weight] * 4 + [rows] * 8 + [pltpu.SemaphoreType.DMA((4,))],
        compiler_params=pltpu.CompilerParams(vmem_limit_bytes=VMEM_LIMIT),
        cost_estimate=pl.CostEstimate(
            flops=20_000_000_000, bytes_accessed=16_000_000, transcendentals=2_000_000
        ),
        name="temporal",
    )(r, wo, wq, wk, wv)


def native(rows, half):
    return lax.broadcasted_iota(jnp.int32, (rows, 128), 1) // 64 == half


def rolled(x):
    return pltpu.roll(x.astype(F32), 64, 1).astype(BF)


def pack_rows(x, half, put):
    for b in range(4):
        tile = b + 5 * half
        put(b * 64, x[:, tile * 128 : tile * 128 + 128])
    shared = x[:, 512:640]
    put(256, jnp.where(native(32, half), shared[:32], rolled(shared[32:])))


def pack_kernel(*refs):
    *in_refs, out_ref = refs
    for f in range(8):
        for a, ref in enumerate(in_refs):
            for half in range(2):

                def put(row, value):
                    out_ref[f, half, a, row : row + value.shape[0]] = value

                pack_rows(ref[f], half, put)


def pack(*arrays):
    vmem = pl.BlockSpec(memory_space=pltpu.VMEM)
    return pl.pallas_call(
        pack_kernel,
        out_shape=jax.ShapeDtypeStruct((8, 2, len(arrays), ROWS, 128), BF),
        in_specs=[vmem] * len(arrays),
        out_specs=vmem,
        compiler_params=pltpu.CompilerParams(vmem_limit_bytes=32 * 1024 * 1024),
        name="pack",
    )(*arrays)


def project_kernel(m_ref, w_ref, v_ref, middle_ref, vg_ref):
    row = lax.broadcasted_iota(jnp.int32, (512, 512), 0)
    column = lax.broadcasted_iota(jnp.int32, (512, 512), 1)
    frame, block, low = row // 64, (row // 8) % 8, row % 8
    perm = (column == block * 64 + frame * 8 + low).astype(BF)
    middle = nn(perm, m_ref[...].reshape(512, D)).astype(BF)
    middle_ref[...] = middle.reshape(8, 64, D)
    gs = nt(middle, w_ref[...]).astype(BF)
    for f in range(8):
        for a, x in enumerate((v_ref[f], gs[f * 64 : f * 64 + 64])):
            for half in range(2):

                def put(row, value):
                    vg_ref[f, half, a, row : row + value.shape[0]] = value

                pack_rows(x, half, put)


def project(m, w, v):
    vmem = pl.BlockSpec(memory_space=pltpu.VMEM)
    return pl.pallas_call(
        project_kernel,
        out_shape=(
            jax.ShapeDtypeStruct((8, 64, D), BF),
            jax.ShapeDtypeStruct((8, 2, 2, ROWS, 128), BF),
        ),
        in_specs=[vmem, vmem, vmem],
        out_specs=(vmem, vmem),
        compiler_params=pltpu.CompilerParams(vmem_limit_bytes=VMEM_LIMIT),
        cost_estimate=pl.CostEstimate(
            flops=4_000_000_000, bytes_accessed=8_000_000, transcendentals=0
        ),
        name="project",
    )(m, w, v)


def expand(dst, ref, a, half):
    for b in range(4):
        dst[b + half] = ref[:, a, b * 64 : b * 64 + 64].reshape(1024, 128)
    shared = ref[:, a, 256:288].reshape(512, 128)
    both = [x.reshape(16, 32, 128) for x in (shared, rolled(shared))]
    dst[4 * (1 - half)] = jnp.concatenate(both, axis=1).reshape(1024, 128)


def collapse(ref, a, src, half):
    for b in range(4):
        ref[:, a, b * 64 : b * 64 + 64] = src[b + half].reshape(16, 64, 128)
    shared = src[4 * (1 - half)].reshape(16, 64, 128)
    low, high = shared[:, :32].reshape(512, 128), shared[:, 32:].reshape(512, 128)
    both = jnp.where(native(512, half), low, rolled(high))
    ref[:, a, 256:288] = both.reshape(16, 32, 128)


def head_window(j, half):
    return j // 2, 64 * half + j * HEAD_DIM - (j // 2) * 128


def tiles(ref, t, rows=slice(None)):
    return jnp.concatenate([ref[t, rows], ref[t + 1, rows]], axis=1)


def masked(x, mask):
    return jnp.where(mask, x, jnp.zeros_like(x))


def put_tiles(ref, t, new, mask):
    new = new.astype(BF)
    for side in range(2):
        lanes = slice(side * 128, side * 128 + 128)
        ref[t + side] = jnp.where(mask[:, lanes], new[:, lanes], ref[t + side])


def probs_kernel(half_ref, qk_ref, p_ref, q, k, kh):
    half, j = half_ref[0], pl.program_id(0)

    @pl.when(j == 0)
    def _():
        expand(q, qk_ref, 0, half)
        expand(k, qk_ref, 1, half)

    t, low = head_window(j, half)
    kh[...] = masked(tiles(k, t), lane_mask(1024, low))
    for i in range(4):
        rows = slice(i * 256, (i + 1) * 256)
        s = nt(kh[...], tiles(q, t, rows)) * (SCALE * LOG2E)
        p = jnp.exp2(s - jnp.max(s, axis=0, keepdims=True))
        p_ref[0, :, rows] = (p * (1.0 / jnp.sum(p, axis=0, keepdims=True))).astype(BF)


def fixed(arrays):
    return pl.BlockSpec((16, arrays, ROWS, 128), lambda j: (0, 0, 0, 0))


SCALAR = pl.BlockSpec(memory_space=pltpu.SMEM)
EACH_HEAD = pl.BlockSpec((1, 1024, 1024), lambda j: (j, 0, 0))
TILES = pltpu.VMEM((5, 1024, 128), BF)
WINDOW = pltpu.VMEM((1024, 256), BF)


def probs(half, qk):
    return pl.pallas_call(
        probs_kernel,
        out_shape=jax.ShapeDtypeStruct((8, 1024, 1024), BF),
        grid=(8,),
        in_specs=[SCALAR, fixed(2)],
        out_specs=EACH_HEAD,
        scratch_shapes=[TILES, TILES, WINDOW],
        compiler_params=pltpu.CompilerParams(vmem_limit_bytes=VMEM_LIMIT),
        cost_estimate=pl.CostEstimate(
            flops=20_000_000_000, bytes_accessed=20_000_000, transcendentals=8_400_000
        ),
        name="probs",
    )(half, qk)


def value_kernel(half_ref, vg_ref, p_ref, out_ref, g, dv):
    half, j = half_ref[0], pl.program_id(0)

    @pl.when(j == 0)
    def _():
        expand(g, vg_ref, 1, half)

    t, low = head_window(j, half)
    put_tiles(dv, t, nn(p_ref[0], tiles(g, t)), lane_mask(1024, low))

    @pl.when(j == 7)
    def _():
        collapse(out_ref, 0, dv, half)


def value_grads(half, vg, p):
    return pl.pallas_call(
        value_kernel,
        out_shape=jax.ShapeDtypeStruct((16, 1, ROWS, 128), BF),
        grid=(8,),
        in_specs=[SCALAR, fixed(2), EACH_HEAD],
        out_specs=fixed(1),
        scratch_shapes=[TILES, TILES],
        compiler_params=pltpu.CompilerParams(vmem_limit_bytes=VMEM_LIMIT),
        cost_estimate=pl.CostEstimate(
            flops=5_000_000_000, bytes_accessed=20_000_000, transcendentals=0
        ),
        name="value_grads",
    )(half, vg, p)


def grads_kernel(half_ref, qk_ref, vg_ref, p_ref, out_ref, q, k, v, g, dq, dk, kh, vh, ds):
    half, j = half_ref[0], pl.program_id(0)

    @pl.when(j == 0)
    def _():
        for dst, ref, a in ((q, qk_ref, 0), (k, qk_ref, 1), (v, vg_ref, 0), (g, vg_ref, 1)):
            expand(dst, ref, a, half)

    t, low = head_window(j, half)
    mask = lane_mask(1024, low)
    kh[...] = tiles(k, t)
    vh[...] = masked(tiles(v, t), mask)
    for i in range(4):
        rows = slice(i * 256, (i + 1) * 256)
        dp = nt(vh[...], tiles(g, t, rows))
        p = p_ref[0, :, rows].astype(F32)
        delta = jnp.sum(p * dp, axis=0, keepdims=True)
        ds[:, rows] = (p * (dp - delta)).astype(BF)
    put_tiles(dk, t, nn(ds[...], tiles(q, t)) * SCALE, mask)
    put_tiles(dq, t, tn(ds[...], kh[...]) * SCALE, mask)

    @pl.when(j == 7)
    def _():
        collapse(out_ref, 0, dq, half)
        collapse(out_ref, 1, dk, half)


def grads(half, qk, vg, p):
    return pl.pallas_call(
        grads_kernel,
        out_shape=jax.ShapeDtypeStruct((16, 2, ROWS, 128), BF),
        grid=(8,),
        in_specs=[SCALAR, fixed(2), fixed(2), EACH_HEAD],
        out_specs=fixed(2),
        scratch_shapes=[TILES] * 6 + [WINDOW, WINDOW, pltpu.VMEM((1024, 1024), BF)],
        compiler_params=pltpu.CompilerParams(vmem_limit_bytes=VMEM_LIMIT),
        cost_estimate=pl.CostEstimate(
            flops=20_000_000_000, bytes_accessed=26_000_000, transcendentals=0
        ),
        name="grads",
    )(half, qk, vg, p)


def unpack_kernel(qk_ref, v_ref, *out_refs):
    for f in range(8):
        for out, ref, a in zip(out_refs, (qk_ref, qk_ref, v_ref), (0, 1, 0)):
            for half in range(2):
                for b in range(4):
                    lane = (b + 5 * half) * 128
                    out[f, :, lane : lane + 128] = ref[f, half, a, b * 64 : b * 64 + 64]
            first, second = ref[f, 0, a, 256:288], ref[f, 1, a, 256:288]
            left = native(32, 0)
            out[f, :32, 512:640] = jnp.where(left, first, second)
            out[f, 32:, 512:640] = rolled(jnp.where(left, second, first))


def unpack(qk, v):
    whole = jax.ShapeDtypeStruct((8, 64, D), BF)
    vmem = pl.BlockSpec(memory_space=pltpu.VMEM)
    return pl.pallas_call(
        unpack_kernel,
        out_shape=(whole,) * 3,
        in_specs=[vmem, vmem],
        out_specs=(vmem,) * 3,
        compiler_params=pltpu.CompilerParams(vmem_limit_bytes=32 * 1024 * 1024),
        name="unpack",
    )(qk, v)


def exchange(x, axis):
    return lax.all_to_all(x, axis, 0, 0, tiled=True)


def per_device(
    query_time, key_time, value_time, query_space, key_space, value_space, grad_output,
    outproj_time, queryproj_time, keyproj_time, valueproj_time, outproj_space,
):
    half = (lax.axis_index("space") % 2).astype(jnp.int32).reshape(1)
    qk = pack(query_space, key_space)
    t = jnp.stack([query_time, key_time, value_time, grad_output])
    t = t.reshape(4, 8, 8, 8, D).transpose(2, 0, 1, 3, 4).reshape(8, 4, 64, D)
    t, qk = lax.optimization_barrier((t, qk))
    t = exchange(t, "tm")
    qk, t = lax.optimization_barrier((qk, t))
    qk = exchange(qk.reshape(16, 2, ROWS, 128), "space")
    middle = temporal(t, outproj_time, queryproj_time, keyproj_time, valueproj_time)
    middle, qk = lax.optimization_barrier((middle, qk))
    middle = exchange(middle, "tm")
    middle_grad, vg = project(middle, outproj_space, value_space)
    vg, qk = lax.optimization_barrier((vg, qk))
    p = probs(half, qk)
    vg = exchange(vg.reshape(16, 2, ROWS, 128), "space")
    dv = value_grads(half, vg, p)
    dv, qk = lax.optimization_barrier((dv, qk))
    out_v = exchange(dv, "space")
    dqk = grads(half, qk, vg, p)
    dqk, out_v = lax.optimization_barrier((dqk, out_v))
    out_qk = exchange(dqk, "space")
    query_grad, key_grad, value_grad = unpack(
        out_qk.reshape(8, 2, 2, ROWS, 128), out_v.reshape(8, 2, 1, ROWS, 128)
    )
    return query_grad, key_grad, value_grad, middle_grad


def solution(mesh):
    bulk = P("tm", "space", None)
    return jax.shard_map(
        per_device,
        mesh=mesh,
        in_specs=(bulk,) * 7 + (P(),) * 5,
        out_specs=(bulk,) * 4,
        check_vma=False,
    )
```

```python
import jax
import jax.numpy as jnp
from jax import lax
from jax.experimental import pallas as pl
from jax.experimental.pallas import tpu as pltpu
from jax.sharding import PartitionSpec as P

HEAD_DIM = 72
D = 1152
ROWS = 288
SCALE = HEAD_DIM**-0.5
LOG2E = 1.4426950408889634
BF = jnp.bfloat16
F32 = jnp.float32
VMEM_LIMIT = 56 * 1024 * 1024


def nn(a, b):
    return lax.dot_general(a, b, (((1,), (0,)), ((), ())), preferred_element_type=F32)


def nt(a, b):
    return lax.dot_general(a, b, (((1,), (1,)), ((), ())), preferred_element_type=F32)


def tn(a, b):
    return lax.dot_general(a, b, (((0,), (0,)), ((), ())), preferred_element_type=F32)


def lane_mask(rows, low):
    lane = lax.broadcasted_iota(jnp.int32, (rows, 256), 1)
    return (lane >= low) & (lane < low + HEAD_DIM)


def permutation(inner):
    outer = 512 // inner
    row = lax.broadcasted_iota(jnp.int32, (512, 512), 0)
    column = lax.broadcasted_iota(jnp.int32, (512, 512), 1)
    return (column == inner * (row % outer) + row // outer).astype(BF)


def temporal_kernel(
    r_ref, wo_hbm, wq_hbm, wk_hbm, wv_hbm, out_ref,
    wo, wq, wk, wv, q, k, v, g0, g, dq, dk, dv, sems,
):
    copies = [
        pltpu.make_async_copy(src, dst, sems.at[i])
        for i, (src, dst) in enumerate(((wo_hbm, wo), (wq_hbm, wq), (wk_hbm, wk), (wv_hbm, wv)))
    ]
    for copy in copies:
        copy.start()
    to_patch = permutation(8)
    for a, dst in enumerate((q, k, v, g0)):
        dst[...] = nn(to_patch, r_ref[:, a].reshape(512, D)).astype(BF)
    copies[0].wait()
    g[...] = nt(g0[...], wo[...]).astype(BF)
    same = (
        lax.broadcasted_iota(jnp.int32, (2, 128, 128), 1) // 64
        == lax.broadcasted_iota(jnp.int32, (2, 128, 128), 2) // 64
    )

    def pair(i, carry):
        first = i * 2 * HEAD_DIM // 128 * 128
        window = pl.ds(pl.multiple_of(first, 128), 256)
        low = i * 2 * HEAD_DIM - first
        masks = [lane_mask(128, low), lane_mask(128, low + HEAD_DIM)]
        either = masks[0] | masks[1]

        def stacked(x):
            return jnp.concatenate([jnp.where(mask, x, jnp.zeros_like(x)) for mask in masks])

        def beside(x):
            return jnp.concatenate([x[0], x[1]], axis=1)

        for b in range(4):
            rows = pl.ds(b * 128, 128)
            qb, kb, vb, gb = [ref[rows, window] for ref in (q, k, v, g)]
            kh = stacked(kb)
            s = nt(kh, qb).reshape(2, 128, 128) * (SCALE * LOG2E)
            s = jnp.where(same, s, -1e30)
            p = jnp.exp2(s - jnp.max(s, axis=1, keepdims=True))
            p = p * (1.0 / jnp.sum(p, axis=1, keepdims=True))
            dp = nt(stacked(vb), gb).reshape(2, 128, 128)
            delta = jnp.sum(p * dp, axis=1, keepdims=True)
            ds = (p * (dp - delta)).astype(BF)
            new_dk = (nn(beside(ds), stacked(qb)) * SCALE).astype(BF)
            new_dv = nn(beside(p.astype(BF)), stacked(gb)).astype(BF)
            new_dq = (tn(ds.reshape(256, 128), kh) * SCALE).astype(BF)
            for ref, new in ((dq, new_dq), (dk, new_dk), (dv, new_dv)):
                ref[rows, window] = jnp.where(either, new, ref[rows, window])
        return carry

    lax.fori_loop(0, D // HEAD_DIM // 2, pair, 0)
    for copy in copies[1:]:
        copy.wait()
    middle = (
        g0[...].astype(F32)
        + nt(dq[...], wq[...])
        + nt(dk[...], wk[...])
        + nt(dv[...], wv[...])
    ).astype(BF)
    out_ref[...] = nn(permutation(64), middle).astype(BF).reshape(8, 64, D)


def temporal(r, wo, wq, wk, wv):
    hbm = pl.BlockSpec(memory_space=pl.ANY)
    vmem = pl.BlockSpec(memory_space=pltpu.VMEM)
    weight = pltpu.VMEM((D, D), BF)
    rows = pltpu.VMEM((512, D), BF)
    return pl.pallas_call(
        temporal_kernel,
        out_shape=jax.ShapeDtypeStruct((8, 64, D), BF),
        in_specs=[vmem, hbm, hbm, hbm, hbm],
        out_specs=vmem,
        scratch_shapes=[weight] * 4 + [rows] * 8 + [pltpu.SemaphoreType.DMA((4,))],
        compiler_params=pltpu.CompilerParams(vmem_limit_bytes=VMEM_LIMIT),
        cost_estimate=pl.CostEstimate(
            flops=20_000_000_000, bytes_accessed=16_000_000, transcendentals=2_000_000
        ),
        name="temporal",
    )(r, wo, wq, wk, wv)


def native(rows, half):
    return lax.broadcasted_iota(jnp.int32, (rows, 128), 1) // 64 == half


def rolled(x):
    return pltpu.roll(x.astype(F32), 64, 1).astype(BF)


def pack_rows(x, half, put):
    for b in range(4):
        tile = b + 5 * half
        put(b * 64, x[:, tile * 128 : tile * 128 + 128])
    shared = x[:, 512:640]
    put(256, jnp.where(native(32, half), shared[:32], rolled(shared[32:])))


def pack_kernel(*refs):
    *in_refs, out_ref = refs
    for f in range(8):
        for a, ref in enumerate(in_refs):
            for half in range(2):

                def put(row, value):
                    out_ref[f, half, a, row : row + value.shape[0]] = value

                pack_rows(ref[f], half, put)


def pack(*arrays):
    vmem = pl.BlockSpec(memory_space=pltpu.VMEM)
    return pl.pallas_call(
        pack_kernel,
        out_shape=jax.ShapeDtypeStruct((8, 2, len(arrays), ROWS, 128), BF),
        in_specs=[vmem] * len(arrays),
        out_specs=vmem,
        compiler_params=pltpu.CompilerParams(vmem_limit_bytes=32 * 1024 * 1024),
        name="pack",
    )(*arrays)


def project_kernel(m_ref, w_ref, v_ref, middle_ref, vg_ref):
    row = lax.broadcasted_iota(jnp.int32, (512, 512), 0)
    column = lax.broadcasted_iota(jnp.int32, (512, 512), 1)
    frame, block, low = row // 64, (row // 8) % 8, row % 8
    perm = (column == block * 64 + frame * 8 + low).astype(BF)
    middle = nn(perm, m_ref[...].reshape(512, D)).astype(BF)
    middle_ref[...] = middle.reshape(8, 64, D)
    gs = nt(middle, w_ref[...]).astype(BF)
    for f in range(8):
        for a, x in enumerate((v_ref[f], gs[f * 64 : f * 64 + 64])):
            for half in range(2):

                def put(row, value):
                    vg_ref[f, half, a, row : row + value.shape[0]] = value

                pack_rows(x, half, put)


def project(m, w, v):
    vmem = pl.BlockSpec(memory_space=pltpu.VMEM)
    return pl.pallas_call(
        project_kernel,
        out_shape=(
            jax.ShapeDtypeStruct((8, 64, D), BF),
            jax.ShapeDtypeStruct((8, 2, 2, ROWS, 128), BF),
        ),
        in_specs=[vmem, vmem, vmem],
        out_specs=(vmem, vmem),
        compiler_params=pltpu.CompilerParams(vmem_limit_bytes=32 * 1024 * 1024),
        cost_estimate=pl.CostEstimate(
            flops=4_000_000_000, bytes_accessed=8_000_000, transcendentals=0
        ),
        name="project",
    )(m, w, v)


def expand(dst, ref, a, half):
    for b in range(4):
        dst[b + half] = ref[:, a, b * 64 : b * 64 + 64].reshape(1024, 128)
    shared = ref[:, a, 256:288].reshape(512, 128)
    both = [x.reshape(16, 32, 128) for x in (shared, rolled(shared))]
    dst[4 * (1 - half)] = jnp.concatenate(both, axis=1).reshape(1024, 128)


def collapse(ref, a, src, half):
    for b in range(4):
        ref[:, a, b * 64 : b * 64 + 64] = src[b + half].reshape(16, 64, 128)
    shared = src[4 * (1 - half)].reshape(16, 64, 128)
    low, high = shared[:, :32].reshape(512, 128), shared[:, 32:].reshape(512, 128)
    both = jnp.where(native(512, half), low, rolled(high))
    ref[:, a, 256:288] = both.reshape(16, 32, 128)


def head_window(j, half):
    return j // 2, 64 * half + j * HEAD_DIM - (j // 2) * 128


def tiles(ref, t, rows=slice(None)):
    return jnp.concatenate([ref[t, rows], ref[t + 1, rows]], axis=1)


def masked(x, mask):
    return jnp.where(mask, x, jnp.zeros_like(x))


def put_tiles(ref, t, new, mask):
    new = new.astype(BF)
    for side in range(2):
        lanes = slice(side * 128, side * 128 + 128)
        ref[t + side] = jnp.where(mask[:, lanes], new[:, lanes], ref[t + side])


def probs_kernel(half_ref, qk_ref, p_ref, q, k, kh):
    half, j = half_ref[0], pl.program_id(0)

    @pl.when(j == 0)
    def _():
        expand(q, qk_ref, 0, half)
        expand(k, qk_ref, 1, half)

    t, low = head_window(j, half)
    kh[...] = masked(tiles(k, t), lane_mask(1024, low))
    for i in range(4):
        rows = slice(i * 256, (i + 1) * 256)
        s = nt(kh[...], tiles(q, t, rows)) * (SCALE * LOG2E)
        p = jnp.exp2(s - jnp.max(s, axis=0, keepdims=True))
        p_ref[0, :, rows] = (p * (1.0 / jnp.sum(p, axis=0, keepdims=True))).astype(BF)


SCALAR = pl.BlockSpec(memory_space=pltpu.SMEM)
VMEM = pl.BlockSpec(memory_space=pltpu.VMEM)
TILES = pltpu.VMEM((5, 1024, 128), BF)
WINDOW = pltpu.VMEM((1024, 256), BF)
EACH_HEAD = pl.BlockSpec((1, 1024, 1024), lambda j: (j, 0, 0))


def fixed(arrays):
    return pl.BlockSpec((16, arrays, ROWS, 128), lambda j: (0, 0, 0, 0))


def probs(half, qk):
    return pl.pallas_call(
        probs_kernel,
        out_shape=jax.ShapeDtypeStruct((8, 1024, 1024), BF),
        grid=(8,),
        in_specs=[SCALAR, fixed(2)],
        out_specs=EACH_HEAD,
        scratch_shapes=[TILES, TILES, WINDOW],
        compiler_params=pltpu.CompilerParams(vmem_limit_bytes=VMEM_LIMIT),
        cost_estimate=pl.CostEstimate(
            flops=20_000_000_000, bytes_accessed=20_000_000, transcendentals=8_400_000
        ),
        name="probs",
    )(half, qk)


def grads_kernel(
    half_ref, qk_ref, vg_ref, p_ref, out_ref, q, k, v, g, dq, dk, dv, kh, vh, ds
):
    half, j = half_ref[0], pl.program_id(0)

    @pl.when(j == 0)
    def _():
        for dst, ref, a in ((q, qk_ref, 0), (k, qk_ref, 1), (v, vg_ref, 0), (g, vg_ref, 1)):
            expand(dst, ref, a, half)

    t, low = head_window(j, half)
    mask = lane_mask(1024, low)
    kh[...] = tiles(k, t)
    vh[...] = masked(tiles(v, t), mask)
    for i in range(4):
        rows = slice(i * 256, (i + 1) * 256)
        dp = nt(vh[...], tiles(g, t, rows))
        p = p_ref[0, :, rows].astype(F32)
        delta = jnp.sum(p * dp, axis=0, keepdims=True)
        ds[:, rows] = (p * (dp - delta)).astype(BF)
    put_tiles(dv, t, nn(p_ref[0], tiles(g, t)), mask)
    put_tiles(dk, t, nn(ds[...], tiles(q, t)) * SCALE, mask)
    put_tiles(dq, t, tn(ds[...], kh[...]) * SCALE, mask)

    @pl.when(j == 7)
    def _():
        for a, src in enumerate((dq, dk, dv)):
            collapse(out_ref, a, src, half)


def grads(half, qk, vg, p):
    return pl.pallas_call(
        grads_kernel,
        out_shape=jax.ShapeDtypeStruct((16, 3, ROWS, 128), BF),
        grid=(8,),
        in_specs=[SCALAR, fixed(2), fixed(2), EACH_HEAD],
        out_specs=fixed(3),
        scratch_shapes=[TILES] * 7 + [WINDOW, WINDOW, pltpu.VMEM((1024, 1024), BF)],
        compiler_params=pltpu.CompilerParams(vmem_limit_bytes=VMEM_LIMIT),
        cost_estimate=pl.CostEstimate(
            flops=25_000_000_000, bytes_accessed=26_000_000, transcendentals=0
        ),
        name="grads",
    )(half, qk, vg, p)


def unpack_kernel(r_ref, *out_refs):
    for f in range(8):
        for a, out in enumerate(out_refs):
            for half in range(2):
                for b in range(4):
                    lane = (b + 5 * half) * 128
                    out[f, :, lane : lane + 128] = r_ref[f, half, a, b * 64 : b * 64 + 64]
            first, second = r_ref[f, 0, a, 256:288], r_ref[f, 1, a, 256:288]
            left = native(32, 0)
            out[f, :32, 512:640] = jnp.where(left, first, second)
            out[f, 32:, 512:640] = rolled(jnp.where(left, second, first))


def unpack(r):
    whole = jax.ShapeDtypeStruct((8, 64, D), BF)
    vmem = pl.BlockSpec(memory_space=pltpu.VMEM)
    return pl.pallas_call(
        unpack_kernel,
        out_shape=(whole,) * 3,
        in_specs=[vmem],
        out_specs=(vmem,) * 3,
        compiler_params=pltpu.CompilerParams(vmem_limit_bytes=32 * 1024 * 1024),
        name="unpack",
    )(r)


def exchange(x, axis):
    return lax.all_to_all(x, axis, 0, 0, tiled=True)


def per_device(
    query_time, key_time, value_time, query_space, key_space, value_space, grad_output,
    outproj_time, queryproj_time, keyproj_time, valueproj_time, outproj_space,
):
    half = (lax.axis_index("space") % 2).astype(jnp.int32).reshape(1)
    qk = pack(query_space, key_space)
    t = jnp.stack([query_time, key_time, value_time, grad_output])
    t = t.reshape(4, 8, 8, 8, D).transpose(2, 0, 1, 3, 4).reshape(8, 4, 64, D)
    t, qk = lax.optimization_barrier((t, qk))
    t = exchange(t, "tm")
    qk, t = lax.optimization_barrier((qk, t))
    qk = exchange(qk.reshape(16, 2, ROWS, 128), "space")
    middle = temporal(t, outproj_time, queryproj_time, keyproj_time, valueproj_time)
    middle, qk = lax.optimization_barrier((middle, qk))
    middle = exchange(middle, "tm")
    middle_grad, vg = project(middle, outproj_space, value_space)
    vg, qk = lax.optimization_barrier((vg, qk))
    p = probs(half, qk)
    vg = exchange(vg.reshape(16, 2, ROWS, 128), "space")
    out = exchange(grads(half, qk, vg, p), "space")
    query_grad, key_grad, value_grad = unpack(out.reshape(8, 2, 3, ROWS, 128))
    return query_grad, key_grad, value_grad, middle_grad


def solution(mesh):
    bulk = P("tm", "space", None)
    return jax.shard_map(
        per_device,
        mesh=mesh,
        in_specs=(bulk,) * 7 + (P(),) * 5,
        out_specs=(bulk,) * 4,
        check_vma=False,
    )
```

```python
import jax
import jax.numpy as jnp
from jax import lax
from jax.experimental import pallas as pl
from jax.experimental.pallas import tpu as pltpu
from jax.sharding import PartitionSpec as P

HEAD_DIM = 72
D = 1152
ROWS = 288
SCALE = HEAD_DIM**-0.5
LOG2E = 1.4426950408889634
BF = jnp.bfloat16
F32 = jnp.float32
VMEM_LIMIT = 56 * 1024 * 1024


def nn(a, b):
    return lax.dot_general(a, b, (((1,), (0,)), ((), ())), preferred_element_type=F32)


def nt(a, b):
    return lax.dot_general(a, b, (((1,), (1,)), ((), ())), preferred_element_type=F32)


def tn(a, b):
    return lax.dot_general(a, b, (((0,), (0,)), ((), ())), preferred_element_type=F32)


def lane_mask(rows, low):
    lane = lax.broadcasted_iota(jnp.int32, (rows, 256), 1)
    return (lane >= low) & (lane < low + HEAD_DIM)


def permutation(inner):
    outer = 512 // inner
    row = lax.broadcasted_iota(jnp.int32, (512, 512), 0)
    column = lax.broadcasted_iota(jnp.int32, (512, 512), 1)
    return (column == inner * (row % outer) + row // outer).astype(BF)


def temporal_kernel(
    r_ref, wo_hbm, wq_hbm, wk_hbm, wv_hbm, out_ref,
    wo, wq, wk, wv, q, k, v, g0, g, dq, dk, dv, sems,
):
    copies = [
        pltpu.make_async_copy(src, dst, sems.at[i])
        for i, (src, dst) in enumerate(((wo_hbm, wo), (wq_hbm, wq), (wk_hbm, wk), (wv_hbm, wv)))
    ]
    for copy in copies:
        copy.start()
    to_patch = permutation(8)
    for a, dst in enumerate((q, k, v, g0)):
        dst[...] = nn(to_patch, r_ref[:, a].reshape(512, D)).astype(BF)
    copies[0].wait()
    g[...] = nt(g0[...], wo[...]).astype(BF)
    same = (
        lax.broadcasted_iota(jnp.int32, (2, 128, 128), 1) // 64
        == lax.broadcasted_iota(jnp.int32, (2, 128, 128), 2) // 64
    )

    def pair(i, carry):
        first = i * 2 * HEAD_DIM // 128 * 128
        window = pl.ds(pl.multiple_of(first, 128), 256)
        low = i * 2 * HEAD_DIM - first
        masks = [lane_mask(128, low), lane_mask(128, low + HEAD_DIM)]
        either = masks[0] | masks[1]

        def stacked(x):
            return jnp.concatenate([jnp.where(mask, x, jnp.zeros_like(x)) for mask in masks])

        def beside(x):
            return jnp.concatenate([x[0], x[1]], axis=1)

        for b in range(4):
            rows = pl.ds(b * 128, 128)
            qb, kb, vb, gb = [ref[rows, window] for ref in (q, k, v, g)]
            kh = stacked(kb)
            s = nt(kh, qb).reshape(2, 128, 128) * (SCALE * LOG2E)
            s = jnp.where(same, s, -1e30)
            p = jnp.exp2(s - jnp.max(s, axis=1, keepdims=True))
            p = p * (1.0 / jnp.sum(p, axis=1, keepdims=True))
            dp = nt(stacked(vb), gb).reshape(2, 128, 128)
            delta = jnp.sum(p * dp, axis=1, keepdims=True)
            ds = (p * (dp - delta)).astype(BF)
            new_dk = (nn(beside(ds), stacked(qb)) * SCALE).astype(BF)
            new_dv = nn(beside(p.astype(BF)), stacked(gb)).astype(BF)
            new_dq = (tn(ds.reshape(256, 128), kh) * SCALE).astype(BF)
            for ref, new in ((dq, new_dq), (dk, new_dk), (dv, new_dv)):
                ref[rows, window] = jnp.where(either, new, ref[rows, window])
        return carry

    lax.fori_loop(0, D // HEAD_DIM // 2, pair, 0)
    for copy in copies[1:]:
        copy.wait()
    middle = (
        g0[...].astype(F32)
        + nt(dq[...], wq[...])
        + nt(dk[...], wk[...])
        + nt(dv[...], wv[...])
    ).astype(BF)
    out_ref[...] = nn(permutation(64), middle).astype(BF).reshape(8, 64, D)


def temporal(r, wo, wq, wk, wv):
    hbm = pl.BlockSpec(memory_space=pl.ANY)
    vmem = pl.BlockSpec(memory_space=pltpu.VMEM)
    weight = pltpu.VMEM((D, D), BF)
    rows = pltpu.VMEM((512, D), BF)
    return pl.pallas_call(
        temporal_kernel,
        out_shape=jax.ShapeDtypeStruct((8, 64, D), BF),
        in_specs=[vmem, hbm, hbm, hbm, hbm],
        out_specs=vmem,
        scratch_shapes=[weight] * 4 + [rows] * 8 + [pltpu.SemaphoreType.DMA((4,))],
        compiler_params=pltpu.CompilerParams(vmem_limit_bytes=VMEM_LIMIT),
        cost_estimate=pl.CostEstimate(
            flops=20_000_000_000, bytes_accessed=16_000_000, transcendentals=2_000_000
        ),
        name="temporal",
    )(r, wo, wq, wk, wv)


def native(rows, half):
    return lax.broadcasted_iota(jnp.int32, (rows, 128), 1) // 64 == half


def rolled(x):
    return pltpu.roll(x.astype(F32), 64, 1).astype(BF)


def pack_rows(x, half, put):
    for b in range(4):
        tile = b + 5 * half
        put(b * 64, x[:, tile * 128 : tile * 128 + 128])
    shared = x[:, 512:640]
    put(256, jnp.where(native(32, half), shared[:32], rolled(shared[32:])))


def pack_kernel(*refs):
    *in_refs, out_ref = refs
    for f in range(8):
        for a, ref in enumerate(in_refs):
            for half in range(2):

                def put(row, value):
                    out_ref[f, half, a, row : row + value.shape[0]] = value

                pack_rows(ref[f], half, put)


def pack(*arrays):
    vmem = pl.BlockSpec(memory_space=pltpu.VMEM)
    return pl.pallas_call(
        pack_kernel,
        out_shape=jax.ShapeDtypeStruct((8, 2, len(arrays), ROWS, 128), BF),
        in_specs=[vmem] * len(arrays),
        out_specs=vmem,
        compiler_params=pltpu.CompilerParams(vmem_limit_bytes=32 * 1024 * 1024),
        name="pack",
    )(*arrays)


def project_kernel(m_ref, w_ref, v_ref, middle_ref, vg_ref):
    row = lax.broadcasted_iota(jnp.int32, (512, 512), 0)
    column = lax.broadcasted_iota(jnp.int32, (512, 512), 1)
    frame, block, low = row // 64, (row // 8) % 8, row % 8
    perm = (column == block * 64 + frame * 8 + low).astype(BF)
    middle = nn(perm, m_ref[...].reshape(512, D)).astype(BF)
    middle_ref[...] = middle.reshape(8, 64, D)
    gs = nt(middle, w_ref[...]).astype(BF)
    for f in range(8):
        for a, x in enumerate((v_ref[f], gs[f * 64 : f * 64 + 64])):
            for half in range(2):

                def put(row, value):
                    vg_ref[f, half, a, row : row + value.shape[0]] = value

                pack_rows(x, half, put)


def project(m, w, v):
    vmem = pl.BlockSpec(memory_space=pltpu.VMEM)
    return pl.pallas_call(
        project_kernel,
        out_shape=(
            jax.ShapeDtypeStruct((8, 64, D), BF),
            jax.ShapeDtypeStruct((8, 2, 2, ROWS, 128), BF),
        ),
        in_specs=[vmem, vmem, vmem],
        out_specs=(vmem, vmem),
        compiler_params=pltpu.CompilerParams(vmem_limit_bytes=32 * 1024 * 1024),
        cost_estimate=pl.CostEstimate(
            flops=4_000_000_000, bytes_accessed=8_000_000, transcendentals=0
        ),
        name="project",
    )(m, w, v)


def expand(dst, ref, a, half):
    for b in range(4):
        dst[b + half] = ref[:, a, b * 64 : b * 64 + 64].reshape(1024, 128)
    shared = ref[:, a, 256:288].reshape(512, 128)
    both = [x.reshape(16, 32, 128) for x in (shared, rolled(shared))]
    dst[4 * (1 - half)] = jnp.concatenate(both, axis=1).reshape(1024, 128)


def collapse(ref, a, src, half):
    for b in range(4):
        ref[:, a, b * 64 : b * 64 + 64] = src[b + half].reshape(16, 64, 128)
    shared = src[4 * (1 - half)].reshape(16, 64, 128)
    low, high = shared[:, :32].reshape(512, 128), shared[:, 32:].reshape(512, 128)
    both = jnp.where(native(512, half), low, rolled(high))
    ref[:, a, 256:288] = both.reshape(16, 32, 128)


def head_window(j, half):
    return j // 2, 64 * half + j * HEAD_DIM - (j // 2) * 128


def tiles(ref, t, rows=slice(None)):
    return jnp.concatenate([ref[t, rows], ref[t + 1, rows]], axis=1)


def masked(x, mask):
    return jnp.where(mask, x, jnp.zeros_like(x))


def put_tiles(ref, t, new, mask):
    new = new.astype(BF)
    for side in range(2):
        lanes = slice(side * 128, side * 128 + 128)
        ref[t + side] = jnp.where(mask[:, lanes], new[:, lanes], ref[t + side])


def probs_kernel(half_ref, qk_ref, p_ref, q, k, kh):
    half, j = half_ref[0], pl.program_id(0)

    @pl.when(j == 0)
    def _():
        expand(q, qk_ref, 0, half)
        expand(k, qk_ref, 1, half)

    t, low = head_window(j, half)
    kh[...] = masked(tiles(k, t), lane_mask(1024, low))
    for i in range(4):
        rows = slice(i * 256, (i + 1) * 256)
        s = nt(kh[...], tiles(q, t, rows)) * (SCALE * LOG2E)
        p = jnp.exp2(s - jnp.max(s, axis=0, keepdims=True))
        p_ref[0, :, rows] = (p * (1.0 / jnp.sum(p, axis=0, keepdims=True))).astype(BF)


SCALAR = pl.BlockSpec(memory_space=pltpu.SMEM)
VMEM = pl.BlockSpec(memory_space=pltpu.VMEM)
TILES = pltpu.VMEM((5, 1024, 128), BF)
WINDOW = pltpu.VMEM((1024, 256), BF)
EACH_HEAD = pl.BlockSpec((1, 1024, 1024), lambda j: (j, 0, 0))


def probs(half, qk):
    return pl.pallas_call(
        probs_kernel,
        out_shape=jax.ShapeDtypeStruct((8, 1024, 1024), BF),
        grid=(8,),
        in_specs=[SCALAR, VMEM],
        out_specs=EACH_HEAD,
        scratch_shapes=[TILES, TILES, WINDOW],
        compiler_params=pltpu.CompilerParams(vmem_limit_bytes=44 * 1024 * 1024),
        cost_estimate=pl.CostEstimate(
            flops=20_000_000_000, bytes_accessed=20_000_000, transcendentals=8_400_000
        ),
        name="probs",
    )(half, qk)


def grads_kernel(
    half_ref, qk_ref, vg_ref, p_ref, out_ref, q, k, v, g, dq, dk, dv, kh, vh, ds
):
    half, j = half_ref[0], pl.program_id(0)

    @pl.when(j == 0)
    def _():
        for dst, ref, a in ((q, qk_ref, 0), (k, qk_ref, 1), (v, vg_ref, 0), (g, vg_ref, 1)):
            expand(dst, ref, a, half)

    t, low = head_window(j, half)
    mask = lane_mask(1024, low)
    kh[...] = tiles(k, t)
    vh[...] = masked(tiles(v, t), mask)
    for i in range(4):
        rows = slice(i * 256, (i + 1) * 256)
        dp = nt(vh[...], tiles(g, t, rows))
        p = p_ref[0, :, rows].astype(F32)
        delta = jnp.sum(p * dp, axis=0, keepdims=True)
        ds[:, rows] = (p * (dp - delta)).astype(BF)
    put_tiles(dv, t, nn(p_ref[0], tiles(g, t)), mask)
    put_tiles(dk, t, nn(ds[...], tiles(q, t)) * SCALE, mask)
    put_tiles(dq, t, tn(ds[...], kh[...]) * SCALE, mask)

    @pl.when(j == 7)
    def _():
        for a, src in enumerate((dq, dk, dv)):
            collapse(out_ref, a, src, half)


def grads(half, qk, vg, p):
    return pl.pallas_call(
        grads_kernel,
        out_shape=jax.ShapeDtypeStruct((16, 3, ROWS, 128), BF),
        grid=(8,),
        in_specs=[SCALAR, VMEM, VMEM, EACH_HEAD],
        out_specs=VMEM,
        scratch_shapes=[TILES] * 7 + [WINDOW, WINDOW, pltpu.VMEM((1024, 1024), BF)],
        compiler_params=pltpu.CompilerParams(vmem_limit_bytes=44 * 1024 * 1024),
        cost_estimate=pl.CostEstimate(
            flops=25_000_000_000, bytes_accessed=26_000_000, transcendentals=0
        ),
        name="grads",
    )(half, qk, vg, p)


def unpack_kernel(r_ref, *out_refs):
    for f in range(8):
        for a, out in enumerate(out_refs):
            for half in range(2):
                for b in range(4):
                    lane = (b + 5 * half) * 128
                    out[f, :, lane : lane + 128] = r_ref[f, half, a, b * 64 : b * 64 + 64]
            first, second = r_ref[f, 0, a, 256:288], r_ref[f, 1, a, 256:288]
            left = native(32, 0)
            out[f, :32, 512:640] = jnp.where(left, first, second)
            out[f, 32:, 512:640] = rolled(jnp.where(left, second, first))


def unpack(r):
    whole = jax.ShapeDtypeStruct((8, 64, D), BF)
    vmem = pl.BlockSpec(memory_space=pltpu.VMEM)
    return pl.pallas_call(
        unpack_kernel,
        out_shape=(whole,) * 3,
        in_specs=[vmem],
        out_specs=(vmem,) * 3,
        compiler_params=pltpu.CompilerParams(vmem_limit_bytes=32 * 1024 * 1024),
        name="unpack",
    )(r)


def exchange(x, axis):
    return lax.all_to_all(x, axis, 0, 0, tiled=True)


def per_device(
    query_time, key_time, value_time, query_space, key_space, value_space, grad_output,
    outproj_time, queryproj_time, keyproj_time, valueproj_time, outproj_space,
):
    half = (lax.axis_index("space") % 2).astype(jnp.int32).reshape(1)
    qk = pack(query_space, key_space)
    t = jnp.stack([query_time, key_time, value_time, grad_output])
    t = t.reshape(4, 8, 8, 8, D).transpose(2, 0, 1, 3, 4).reshape(8, 4, 64, D)
    t, qk = lax.optimization_barrier((t, qk))
    t = exchange(t, "tm")
    qk, t = lax.optimization_barrier((qk, t))
    qk = exchange(qk.reshape(16, 2, ROWS, 128), "space")
    middle = temporal(t, outproj_time, queryproj_time, keyproj_time, valueproj_time)
    middle, qk = lax.optimization_barrier((middle, qk))
    middle = exchange(middle, "tm")
    middle_grad, vg = project(middle, outproj_space, value_space)
    vg, qk = lax.optimization_barrier((vg, qk))
    p = probs(half, qk)
    vg = exchange(vg.reshape(16, 2, ROWS, 128), "space")
    out = exchange(grads(half, qk, vg, p), "space")
    query_grad, key_grad, value_grad = unpack(out.reshape(8, 2, 3, ROWS, 128))
    return query_grad, key_grad, value_grad, middle_grad


def solution(mesh):
    bulk = P("tm", "space", None)
    return jax.shard_map(
        per_device,
        mesh=mesh,
        in_specs=(bulk,) * 7 + (P(),) * 5,
        out_specs=(bulk,) * 4,
        check_vma=False,
    )
```

```python
import jax
import jax.numpy as jnp
from jax import lax
from jax.experimental import pallas as pl
from jax.experimental.pallas import tpu as pltpu
from jax.sharding import PartitionSpec as P

HEAD_DIM = 72
D = 1152
ROWS = 288
SCALE = HEAD_DIM**-0.5
LOG2E = 1.4426950408889634
BF = jnp.bfloat16
F32 = jnp.float32
VMEM_LIMIT = 56 * 1024 * 1024


def nn(a, b):
    return lax.dot_general(a, b, (((1,), (0,)), ((), ())), preferred_element_type=F32)


def nt(a, b):
    return lax.dot_general(a, b, (((1,), (1,)), ((), ())), preferred_element_type=F32)


def tn(a, b):
    return lax.dot_general(a, b, (((0,), (0,)), ((), ())), preferred_element_type=F32)


def lane_mask(rows, low):
    lane = lax.broadcasted_iota(jnp.int32, (rows, 256), 1)
    return (lane >= low) & (lane < low + HEAD_DIM)


def permutation(inner):
    outer = 512 // inner
    row = lax.broadcasted_iota(jnp.int32, (512, 512), 0)
    column = lax.broadcasted_iota(jnp.int32, (512, 512), 1)
    return (column == inner * (row % outer) + row // outer).astype(BF)


def temporal_kernel(
    r_ref, wo_hbm, wq_hbm, wk_hbm, wv_hbm, out_ref,
    wo, wq, wk, wv, q, k, v, g0, g, dq, dk, dv, sems,
):
    copies = [
        pltpu.make_async_copy(src, dst, sems.at[i])
        for i, (src, dst) in enumerate(((wo_hbm, wo), (wq_hbm, wq), (wk_hbm, wk), (wv_hbm, wv)))
    ]
    for copy in copies:
        copy.start()
    to_patch = permutation(8)
    for a, dst in enumerate((q, k, v, g0)):
        dst[...] = nn(to_patch, r_ref[:, a].reshape(512, D)).astype(BF)
    copies[0].wait()
    g[...] = nt(g0[...], wo[...]).astype(BF)
    same = (
        lax.broadcasted_iota(jnp.int32, (2, 128, 128), 1) // 64
        == lax.broadcasted_iota(jnp.int32, (2, 128, 128), 2) // 64
    )

    def pair(i, carry):
        first = i * 2 * HEAD_DIM // 128 * 128
        window = pl.ds(pl.multiple_of(first, 128), 256)
        low = i * 2 * HEAD_DIM - first
        masks = [lane_mask(128, low), lane_mask(128, low + HEAD_DIM)]
        either = masks[0] | masks[1]

        def stacked(x):
            return jnp.concatenate([jnp.where(mask, x, jnp.zeros_like(x)) for mask in masks])

        def beside(x):
            return jnp.concatenate([x[0], x[1]], axis=1)

        for b in range(4):
            rows = pl.ds(b * 128, 128)
            qb, kb, vb, gb = [ref[rows, window] for ref in (q, k, v, g)]
            kh = stacked(kb)
            s = nt(kh, qb).reshape(2, 128, 128) * (SCALE * LOG2E)
            s = jnp.where(same, s, -1e30)
            p = jnp.exp2(s - jnp.max(s, axis=1, keepdims=True))
            p = p * (1.0 / jnp.sum(p, axis=1, keepdims=True))
            dp = nt(stacked(vb), gb).reshape(2, 128, 128)
            delta = jnp.sum(p * dp, axis=1, keepdims=True)
            ds = (p * (dp - delta)).astype(BF)
            new_dk = (nn(beside(ds), stacked(qb)) * SCALE).astype(BF)
            new_dv = nn(beside(p.astype(BF)), stacked(gb)).astype(BF)
            new_dq = (tn(ds.reshape(256, 128), kh) * SCALE).astype(BF)
            for ref, new in ((dq, new_dq), (dk, new_dk), (dv, new_dv)):
                ref[rows, window] = jnp.where(either, new, ref[rows, window])
        return carry

    lax.fori_loop(0, D // HEAD_DIM // 2, pair, 0)
    for copy in copies[1:]:
        copy.wait()
    middle = (
        g0[...].astype(F32)
        + nt(dq[...], wq[...])
        + nt(dk[...], wk[...])
        + nt(dv[...], wv[...])
    ).astype(BF)
    out_ref[...] = nn(permutation(64), middle).astype(BF).reshape(8, 64, D)


def temporal(r, wo, wq, wk, wv):
    hbm = pl.BlockSpec(memory_space=pl.ANY)
    vmem = pl.BlockSpec(memory_space=pltpu.VMEM)
    weight = pltpu.VMEM((D, D), BF)
    rows = pltpu.VMEM((512, D), BF)
    return pl.pallas_call(
        temporal_kernel,
        out_shape=jax.ShapeDtypeStruct((8, 64, D), BF),
        in_specs=[vmem, hbm, hbm, hbm, hbm],
        out_specs=vmem,
        scratch_shapes=[weight] * 4 + [rows] * 8 + [pltpu.SemaphoreType.DMA((4,))],
        compiler_params=pltpu.CompilerParams(vmem_limit_bytes=50 * 1024 * 1024),
        cost_estimate=pl.CostEstimate(
            flops=20_000_000_000, bytes_accessed=16_000_000, transcendentals=2_000_000
        ),
        name="temporal",
    )(r, wo, wq, wk, wv)


def native(rows, half):
    return lax.broadcasted_iota(jnp.int32, (rows, 128), 1) // 64 == half


def rolled(x):
    return pltpu.roll(x.astype(F32), 64, 1).astype(BF)


def pack_rows(x, half, put):
    for b in range(4):
        tile = b + 5 * half
        put(b * 64, x[:, tile * 128 : tile * 128 + 128])
    shared = x[:, 512:640]
    put(256, jnp.where(native(32, half), shared[:32], rolled(shared[32:])))


def pack_kernel(*refs):
    *in_refs, out_ref = refs
    for f in range(8):
        for a, ref in enumerate(in_refs):
            for half in range(2):

                def put(row, value):
                    out_ref[f, half, a, row : row + value.shape[0]] = value

                pack_rows(ref[f], half, put)


def pack(*arrays):
    vmem = pl.BlockSpec(memory_space=pltpu.VMEM)
    return pl.pallas_call(
        pack_kernel,
        out_shape=jax.ShapeDtypeStruct((8, 2, len(arrays), ROWS, 128), BF),
        in_specs=[vmem] * len(arrays),
        out_specs=vmem,
        compiler_params=pltpu.CompilerParams(vmem_limit_bytes=32 * 1024 * 1024),
        name="pack",
    )(*arrays)


def project_kernel(m_ref, w_ref, v_ref, middle_ref, vg_ref):
    row = lax.broadcasted_iota(jnp.int32, (512, 512), 0)
    column = lax.broadcasted_iota(jnp.int32, (512, 512), 1)
    frame, block, low = row // 64, (row // 8) % 8, row % 8
    perm = (column == block * 64 + frame * 8 + low).astype(BF)
    middle = nn(perm, m_ref[...].reshape(512, D)).astype(BF)
    middle_ref[...] = middle.reshape(8, 64, D)
    gs = nt(middle, w_ref[...]).astype(BF)
    for f in range(8):
        for a, x in enumerate((v_ref[f], gs[f * 64 : f * 64 + 64])):
            for half in range(2):

                def put(row, value):
                    vg_ref[f, half, a, row : row + value.shape[0]] = value

                pack_rows(x, half, put)


def project(m, w, v):
    vmem = pl.BlockSpec(memory_space=pltpu.VMEM)
    return pl.pallas_call(
        project_kernel,
        out_shape=(
            jax.ShapeDtypeStruct((8, 64, D), BF),
            jax.ShapeDtypeStruct((8, 2, 2, ROWS, 128), BF),
        ),
        in_specs=[vmem, vmem, vmem],
        out_specs=(vmem, vmem),
        compiler_params=pltpu.CompilerParams(vmem_limit_bytes=32 * 1024 * 1024),
        cost_estimate=pl.CostEstimate(
            flops=4_000_000_000, bytes_accessed=8_000_000, transcendentals=0
        ),
        name="project",
    )(m, w, v)


def expand(dst, ref, a, half):
    for b in range(4):
        dst[b + half] = ref[:, a, b * 64 : b * 64 + 64].reshape(1024, 128)
    shared = ref[:, a, 256:288].reshape(512, 128)
    both = [x.reshape(16, 32, 128) for x in (shared, rolled(shared))]
    dst[4 * (1 - half)] = jnp.concatenate(both, axis=1).reshape(1024, 128)


def collapse(ref, a, src, half):
    for b in range(4):
        ref[:, a, b * 64 : b * 64 + 64] = src[b + half].reshape(16, 64, 128)
    shared = src[4 * (1 - half)].reshape(16, 64, 128)
    low, high = shared[:, :32].reshape(512, 128), shared[:, 32:].reshape(512, 128)
    both = jnp.where(native(512, half), low, rolled(high))
    ref[:, a, 256:288] = both.reshape(16, 32, 128)


def head_window(j, half):
    return j // 2, 64 * half + j * HEAD_DIM - (j // 2) * 128


def tiles(ref, t, rows=slice(None)):
    return jnp.concatenate([ref[t, rows], ref[t + 1, rows]], axis=1)


def masked(x, mask):
    return jnp.where(mask, x, jnp.zeros_like(x))


def put_tiles(ref, t, new, mask):
    new = new.astype(BF)
    for side in range(2):
        lanes = slice(side * 128, side * 128 + 128)
        ref[t + side] = jnp.where(mask[:, lanes], new[:, lanes], ref[t + side])


def probs_kernel(half_ref, qk_ref, p_ref, q, k, kh):
    half, j = half_ref[0], pl.program_id(0)

    @pl.when(j == 0)
    def _():
        expand(q, qk_ref, 0, half)
        expand(k, qk_ref, 1, half)

    t, low = head_window(j, half)
    kh[...] = masked(tiles(k, t), lane_mask(1024, low))
    for i in range(4):
        rows = slice(i * 256, (i + 1) * 256)
        s = nt(kh[...], tiles(q, t, rows)) * (SCALE * LOG2E)
        p = jnp.exp2(s - jnp.max(s, axis=0, keepdims=True))
        p_ref[0, :, rows] = (p * (1.0 / jnp.sum(p, axis=0, keepdims=True))).astype(BF)


SCALAR = pl.BlockSpec(memory_space=pltpu.SMEM)
VMEM = pl.BlockSpec(memory_space=pltpu.VMEM)
TILES = pltpu.VMEM((5, 1024, 128), BF)
WINDOW = pltpu.VMEM((1024, 256), BF)
EACH_HEAD = pl.BlockSpec((1, 1024, 1024), lambda j: (j, 0, 0))


def probs(half, qk):
    return pl.pallas_call(
        probs_kernel,
        out_shape=jax.ShapeDtypeStruct((8, 1024, 1024), BF),
        grid=(8,),
        in_specs=[SCALAR, VMEM],
        out_specs=EACH_HEAD,
        scratch_shapes=[TILES, TILES, WINDOW],
        compiler_params=pltpu.CompilerParams(vmem_limit_bytes=44 * 1024 * 1024),
        cost_estimate=pl.CostEstimate(
            flops=20_000_000_000, bytes_accessed=20_000_000, transcendentals=8_400_000
        ),
        name="probs",
    )(half, qk)


def grads_kernel(
    half_ref, qk_ref, vg_ref, p_ref, out_ref, q, k, v, g, dq, dk, dv, kh, vh, ds
):
    half, j = half_ref[0], pl.program_id(0)

    @pl.when(j == 0)
    def _():
        for dst, ref, a in ((q, qk_ref, 0), (k, qk_ref, 1), (v, vg_ref, 0), (g, vg_ref, 1)):
            expand(dst, ref, a, half)

    t, low = head_window(j, half)
    mask = lane_mask(1024, low)
    kh[...] = tiles(k, t)
    vh[...] = masked(tiles(v, t), mask)
    for i in range(4):
        rows = slice(i * 256, (i + 1) * 256)
        dp = nt(vh[...], tiles(g, t, rows))
        p = p_ref[0, :, rows].astype(F32)
        delta = jnp.sum(p * dp, axis=0, keepdims=True)
        ds[:, rows] = (p * (dp - delta)).astype(BF)
    put_tiles(dv, t, nn(p_ref[0], tiles(g, t)), mask)
    put_tiles(dk, t, nn(ds[...], tiles(q, t)) * SCALE, mask)
    put_tiles(dq, t, tn(ds[...], kh[...]) * SCALE, mask)

    @pl.when(j == 7)
    def _():
        for a, src in enumerate((dq, dk, dv)):
            collapse(out_ref, a, src, half)


def grads(half, qk, vg, p):
    return pl.pallas_call(
        grads_kernel,
        out_shape=jax.ShapeDtypeStruct((16, 3, ROWS, 128), BF),
        grid=(8,),
        in_specs=[SCALAR, VMEM, VMEM, EACH_HEAD],
        out_specs=VMEM,
        scratch_shapes=[TILES] * 7 + [WINDOW, WINDOW, pltpu.VMEM((1024, 1024), BF)],
        compiler_params=pltpu.CompilerParams(vmem_limit_bytes=44 * 1024 * 1024),
        cost_estimate=pl.CostEstimate(
            flops=25_000_000_000, bytes_accessed=26_000_000, transcendentals=0
        ),
        name="grads",
    )(half, qk, vg, p)


def unpack_kernel(r_ref, *out_refs):
    for f in range(8):
        for a, out in enumerate(out_refs):
            for half in range(2):
                for b in range(4):
                    lane = (b + 5 * half) * 128
                    out[f, :, lane : lane + 128] = r_ref[f, half, a, b * 64 : b * 64 + 64]
            first, second = r_ref[f, 0, a, 256:288], r_ref[f, 1, a, 256:288]
            left = native(32, 0)
            out[f, :32, 512:640] = jnp.where(left, first, second)
            out[f, 32:, 512:640] = rolled(jnp.where(left, second, first))


def unpack(r):
    whole = jax.ShapeDtypeStruct((8, 64, D), BF)
    vmem = pl.BlockSpec(memory_space=pltpu.VMEM)
    return pl.pallas_call(
        unpack_kernel,
        out_shape=(whole,) * 3,
        in_specs=[vmem],
        out_specs=(vmem,) * 3,
        compiler_params=pltpu.CompilerParams(vmem_limit_bytes=32 * 1024 * 1024),
        name="unpack",
    )(r)


def exchange(x, axis):
    return lax.all_to_all(x, axis, 0, 0, tiled=True)


def per_device(
    query_time, key_time, value_time, query_space, key_space, value_space, grad_output,
    outproj_time, queryproj_time, keyproj_time, valueproj_time, outproj_space,
):
    half = (lax.axis_index("space") % 2).astype(jnp.int32).reshape(1)
    qk = pack(query_space, key_space)
    t = jnp.stack([query_time, key_time, value_time, grad_output])
    t = t.reshape(4, 8, 8, 8, D).transpose(2, 0, 1, 3, 4).reshape(8, 4, 64, D)
    t, qk = lax.optimization_barrier((t, qk))
    t = exchange(t, "tm")
    qk, t = lax.optimization_barrier((qk, t))
    qk = exchange(qk.reshape(16, 2, ROWS, 128), "space")
    middle = temporal(t, outproj_time, queryproj_time, keyproj_time, valueproj_time)
    middle, qk = lax.optimization_barrier((middle, qk))
    middle = exchange(middle, "tm")
    middle_grad, vg = project(middle, outproj_space, value_space)
    vg, qk = lax.optimization_barrier((vg, qk))
    p = probs(half, qk)
    vg = exchange(vg.reshape(16, 2, ROWS, 128), "space")
    out = exchange(grads(half, qk, vg, p), "space")
    query_grad, key_grad, value_grad = unpack(out.reshape(8, 2, 3, ROWS, 128))
    return query_grad, key_grad, value_grad, middle_grad


def solution(mesh):
    bulk = P("tm", "space", None)
    return jax.shard_map(
        per_device,
        mesh=mesh,
        in_specs=(bulk,) * 7 + (P(),) * 5,
        out_specs=(bulk,) * 4,
        check_vma=False,
    )
```

```python
import jax
import jax.numpy as jnp
from jax import lax
from jax.experimental import pallas as pl
from jax.experimental.pallas import tpu as pltpu
from jax.sharding import PartitionSpec as P

HEAD_DIM = 72
D = 1152
ROWS = 288
SCALE = HEAD_DIM**-0.5
LOG2E = 1.4426950408889634
BF = jnp.bfloat16
F32 = jnp.float32
VMEM_LIMIT = 56 * 1024 * 1024


def nn(a, b):
    return lax.dot_general(a, b, (((1,), (0,)), ((), ())), preferred_element_type=F32)


def nt(a, b):
    return lax.dot_general(a, b, (((1,), (1,)), ((), ())), preferred_element_type=F32)


def tn(a, b):
    return lax.dot_general(a, b, (((0,), (0,)), ((), ())), preferred_element_type=F32)


def lane_mask(rows, low):
    lane = lax.broadcasted_iota(jnp.int32, (rows, 256), 1)
    return (lane >= low) & (lane < low + HEAD_DIM)


def permutation(inner):
    outer = 512 // inner
    row = lax.broadcasted_iota(jnp.int32, (512, 512), 0)
    column = lax.broadcasted_iota(jnp.int32, (512, 512), 1)
    return (column == inner * (row % outer) + row // outer).astype(BF)


def temporal_kernel(
    r_ref, wo_hbm, wq_hbm, wk_hbm, wv_hbm, out_ref,
    wo, wq, wk, wv, q, k, v, g0, g, dq, dk, dv, sems,
):
    copies = [
        pltpu.make_async_copy(src, dst, sems.at[i])
        for i, (src, dst) in enumerate(((wo_hbm, wo), (wq_hbm, wq), (wk_hbm, wk), (wv_hbm, wv)))
    ]
    for copy in copies:
        copy.start()
    to_patch = permutation(8)
    for a, dst in enumerate((q, k, v, g0)):
        dst[...] = nn(to_patch, r_ref[:, a].reshape(512, D)).astype(BF)
    copies[0].wait()
    g[...] = nt(g0[...], wo[...]).astype(BF)
    same = (
        lax.broadcasted_iota(jnp.int32, (2, 128, 128), 1) // 64
        == lax.broadcasted_iota(jnp.int32, (2, 128, 128), 2) // 64
    )

    def pair(i, carry):
        first = i * 2 * HEAD_DIM // 128 * 128
        window = pl.ds(pl.multiple_of(first, 128), 256)
        low = i * 2 * HEAD_DIM - first
        masks = [lane_mask(128, low), lane_mask(128, low + HEAD_DIM)]
        either = masks[0] | masks[1]

        def stacked(x):
            return jnp.concatenate([jnp.where(mask, x, jnp.zeros_like(x)) for mask in masks])

        def beside(x):
            return jnp.concatenate([x[0], x[1]], axis=1)

        for b in range(4):
            rows = pl.ds(b * 128, 128)
            qb, kb, vb, gb = [ref[rows, window] for ref in (q, k, v, g)]
            kh = stacked(kb)
            s = nt(kh, qb).reshape(2, 128, 128) * (SCALE * LOG2E)
            s = jnp.where(same, s, -1e30)
            p = jnp.exp2(s - jnp.max(s, axis=1, keepdims=True))
            p = p * (1.0 / jnp.sum(p, axis=1, keepdims=True))
            dp = nt(stacked(vb), gb).reshape(2, 128, 128)
            delta = jnp.sum(p * dp, axis=1, keepdims=True)
            ds = (p * (dp - delta)).astype(BF)
            new_dk = (nn(beside(ds), stacked(qb)) * SCALE).astype(BF)
            new_dv = nn(beside(p.astype(BF)), stacked(gb)).astype(BF)
            new_dq = (tn(ds.reshape(256, 128), kh) * SCALE).astype(BF)
            for ref, new in ((dq, new_dq), (dk, new_dk), (dv, new_dv)):
                ref[rows, window] = jnp.where(either, new, ref[rows, window])
        return carry

    lax.fori_loop(0, D // HEAD_DIM // 2, pair, 0)
    for copy in copies[1:]:
        copy.wait()
    middle = (
        g0[...].astype(F32)
        + nt(dq[...], wq[...])
        + nt(dk[...], wk[...])
        + nt(dv[...], wv[...])
    ).astype(BF)
    out_ref[...] = nn(permutation(64), middle).astype(BF).reshape(8, 64, D)


def temporal(r, wo, wq, wk, wv):
    hbm = pl.BlockSpec(memory_space=pl.ANY)
    vmem = pl.BlockSpec(memory_space=pltpu.VMEM)
    weight = pltpu.VMEM((D, D), BF)
    rows = pltpu.VMEM((512, D), BF)
    return pl.pallas_call(
        temporal_kernel,
        out_shape=jax.ShapeDtypeStruct((8, 64, D), BF),
        in_specs=[vmem, hbm, hbm, hbm, hbm],
        out_specs=vmem,
        scratch_shapes=[weight] * 4 + [rows] * 8 + [pltpu.SemaphoreType.DMA((4,))],
        compiler_params=pltpu.CompilerParams(vmem_limit_bytes=50 * 1024 * 1024),
        cost_estimate=pl.CostEstimate(
            flops=20_000_000_000, bytes_accessed=16_000_000, transcendentals=2_000_000
        ),
        name="temporal",
    )(r, wo, wq, wk, wv)


def native(rows, half):
    return lax.broadcasted_iota(jnp.int32, (rows, 128), 1) // 64 == half


def rolled(x):
    return pltpu.roll(x.astype(F32), 64, 1).astype(BF)


def pack_rows(x, half, put):
    for b in range(4):
        tile = b + 5 * half
        put(b * 64, x[:, tile * 128 : tile * 128 + 128])
    shared = x[:, 512:640]
    put(256, jnp.where(native(32, half), shared[:32], rolled(shared[32:])))


def pack_kernel(*refs):
    *in_refs, out_ref = refs
    for f in range(8):
        for a, ref in enumerate(in_refs):
            for half in range(2):

                def put(row, value):
                    out_ref[f, half, a, row : row + value.shape[0]] = value

                pack_rows(ref[f], half, put)


def pack(*arrays):
    vmem = pl.BlockSpec(memory_space=pltpu.VMEM)
    return pl.pallas_call(
        pack_kernel,
        out_shape=jax.ShapeDtypeStruct((8, 2, len(arrays), ROWS, 128), BF),
        in_specs=[vmem] * len(arrays),
        out_specs=vmem,
        compiler_params=pltpu.CompilerParams(vmem_limit_bytes=60 * 1024 * 1024),
        name="pack",
    )(*arrays)


def project_kernel(m_ref, w_ref, v_ref, middle_ref, vg_ref):
    row = lax.broadcasted_iota(jnp.int32, (512, 512), 0)
    column = lax.broadcasted_iota(jnp.int32, (512, 512), 1)
    frame, block, low = row // 64, (row // 8) % 8, row % 8
    perm = (column == block * 64 + frame * 8 + low).astype(BF)
    middle = nn(perm, m_ref[...].reshape(512, D)).astype(BF)
    middle_ref[...] = middle.reshape(8, 64, D)
    gs = nt(middle, w_ref[...]).astype(BF)
    for f in range(8):
        for a, x in enumerate((v_ref[f], gs[f * 64 : f * 64 + 64])):
            for half in range(2):

                def put(row, value):
                    vg_ref[f, half, a, row : row + value.shape[0]] = value

                pack_rows(x, half, put)


def project(m, w, v):
    vmem = pl.BlockSpec(memory_space=pltpu.VMEM)
    return pl.pallas_call(
        project_kernel,
        out_shape=(
            jax.ShapeDtypeStruct((8, 64, D), BF),
            jax.ShapeDtypeStruct((8, 2, 2, ROWS, 128), BF),
        ),
        in_specs=[vmem, vmem, vmem],
        out_specs=(vmem, vmem),
        compiler_params=pltpu.CompilerParams(vmem_limit_bytes=32 * 1024 * 1024),
        cost_estimate=pl.CostEstimate(
            flops=4_000_000_000, bytes_accessed=8_000_000, transcendentals=0
        ),
        name="project",
    )(m, w, v)


def expand(dst, ref, a, half):
    for b in range(4):
        dst[b + half] = ref[:, a, b * 64 : b * 64 + 64].reshape(1024, 128)
    shared = ref[:, a, 256:288].reshape(512, 128)
    both = [x.reshape(16, 32, 128) for x in (shared, rolled(shared))]
    dst[4 * (1 - half)] = jnp.concatenate(both, axis=1).reshape(1024, 128)


def collapse(ref, a, src, half):
    for b in range(4):
        ref[:, a, b * 64 : b * 64 + 64] = src[b + half].reshape(16, 64, 128)
    shared = src[4 * (1 - half)].reshape(16, 64, 128)
    low, high = shared[:, :32].reshape(512, 128), shared[:, 32:].reshape(512, 128)
    both = jnp.where(native(512, half), low, rolled(high))
    ref[:, a, 256:288] = both.reshape(16, 32, 128)


def head_window(j, half):
    return j // 2, 64 * half + j * HEAD_DIM - (j // 2) * 128


def tiles(ref, t, rows=slice(None)):
    return jnp.concatenate([ref[t, rows], ref[t + 1, rows]], axis=1)


def masked(x, mask):
    return jnp.where(mask, x, jnp.zeros_like(x))


def put_tiles(ref, t, new, mask):
    new = new.astype(BF)
    for side in range(2):
        lanes = slice(side * 128, side * 128 + 128)
        ref[t + side] = jnp.where(mask[:, lanes], new[:, lanes], ref[t + side])


def probs_kernel(half_ref, qk_ref, p_ref, q, k, kh):
    half, j = half_ref[0], pl.program_id(0)

    @pl.when(j == 0)
    def _():
        expand(q, qk_ref, 0, half)
        expand(k, qk_ref, 1, half)

    t, low = head_window(j, half)
    kh[...] = masked(tiles(k, t), lane_mask(1024, low))
    for i in range(4):
        rows = slice(i * 256, (i + 1) * 256)
        s = nt(kh[...], tiles(q, t, rows)) * (SCALE * LOG2E)
        p = jnp.exp2(s - jnp.max(s, axis=0, keepdims=True))
        p_ref[0, :, rows] = (p * (1.0 / jnp.sum(p, axis=0, keepdims=True))).astype(BF)


SCALAR = pl.BlockSpec(memory_space=pltpu.SMEM)
VMEM = pl.BlockSpec(memory_space=pltpu.VMEM)
TILES = pltpu.VMEM((5, 1024, 128), BF)
WINDOW = pltpu.VMEM((1024, 256), BF)
EACH_HEAD = pl.BlockSpec((1, 1024, 1024), lambda j: (j, 0, 0))


def probs(half, qk):
    return pl.pallas_call(
        probs_kernel,
        out_shape=jax.ShapeDtypeStruct((8, 1024, 1024), BF),
        grid=(8,),
        in_specs=[SCALAR, VMEM],
        out_specs=EACH_HEAD,
        scratch_shapes=[TILES, TILES, WINDOW],
        compiler_params=pltpu.CompilerParams(vmem_limit_bytes=44 * 1024 * 1024),
        cost_estimate=pl.CostEstimate(
            flops=20_000_000_000, bytes_accessed=20_000_000, transcendentals=8_400_000
        ),
        name="probs",
    )(half, qk)


def grads_kernel(
    half_ref, qk_ref, vg_ref, p_ref, out_ref, q, k, v, g, dq, dk, dv, kh, vh, ds
):
    half, j = half_ref[0], pl.program_id(0)

    @pl.when(j == 0)
    def _():
        for dst, ref, a in ((q, qk_ref, 0), (k, qk_ref, 1), (v, vg_ref, 0), (g, vg_ref, 1)):
            expand(dst, ref, a, half)

    t, low = head_window(j, half)
    mask = lane_mask(1024, low)
    kh[...] = tiles(k, t)
    vh[...] = masked(tiles(v, t), mask)
    for i in range(4):
        rows = slice(i * 256, (i + 1) * 256)
        dp = nt(vh[...], tiles(g, t, rows))
        p = p_ref[0, :, rows].astype(F32)
        delta = jnp.sum(p * dp, axis=0, keepdims=True)
        ds[:, rows] = (p * (dp - delta)).astype(BF)
    put_tiles(dv, t, nn(p_ref[0], tiles(g, t)), mask)
    put_tiles(dk, t, nn(ds[...], tiles(q, t)) * SCALE, mask)
    put_tiles(dq, t, tn(ds[...], kh[...]) * SCALE, mask)

    @pl.when(j == 7)
    def _():
        for a, src in enumerate((dq, dk, dv)):
            collapse(out_ref, a, src, half)


def grads(half, qk, vg, p):
    return pl.pallas_call(
        grads_kernel,
        out_shape=jax.ShapeDtypeStruct((16, 3, ROWS, 128), BF),
        grid=(8,),
        in_specs=[SCALAR, VMEM, VMEM, EACH_HEAD],
        out_specs=VMEM,
        scratch_shapes=[TILES] * 7 + [WINDOW, WINDOW, pltpu.VMEM((1024, 1024), BF)],
        compiler_params=pltpu.CompilerParams(vmem_limit_bytes=44 * 1024 * 1024),
        cost_estimate=pl.CostEstimate(
            flops=25_000_000_000, bytes_accessed=26_000_000, transcendentals=0
        ),
        name="grads",
    )(half, qk, vg, p)


def unpack_kernel(r_ref, *out_refs):
    for f in range(8):
        for a, out in enumerate(out_refs):
            for half in range(2):
                for b in range(4):
                    lane = (b + 5 * half) * 128
                    out[f, :, lane : lane + 128] = r_ref[f, half, a, b * 64 : b * 64 + 64]
            first, second = r_ref[f, 0, a, 256:288], r_ref[f, 1, a, 256:288]
            left = native(32, 0)
            out[f, :32, 512:640] = jnp.where(left, first, second)
            out[f, 32:, 512:640] = rolled(jnp.where(left, second, first))


def unpack(r):
    whole = jax.ShapeDtypeStruct((8, 64, D), BF)
    vmem = pl.BlockSpec(memory_space=pltpu.VMEM)
    return pl.pallas_call(
        unpack_kernel,
        out_shape=(whole,) * 3,
        in_specs=[vmem],
        out_specs=(vmem,) * 3,
        compiler_params=pltpu.CompilerParams(vmem_limit_bytes=32 * 1024 * 1024),
        name="unpack",
    )(r)


def exchange(x, axis):
    return lax.all_to_all(x, axis, 0, 0, tiled=True)


def per_device(
    query_time, key_time, value_time, query_space, key_space, value_space, grad_output,
    outproj_time, queryproj_time, keyproj_time, valueproj_time, outproj_space,
):
    half = (lax.axis_index("space") % 2).astype(jnp.int32).reshape(1)
    qk = pack(query_space, key_space)
    t = jnp.stack([query_time, key_time, value_time, grad_output])
    t = t.reshape(4, 8, 8, 8, D).transpose(2, 0, 1, 3, 4).reshape(8, 4, 64, D)
    t, qk = lax.optimization_barrier((t, qk))
    t = exchange(t, "tm")
    qk, t = lax.optimization_barrier((qk, t))
    qk = exchange(qk.reshape(16, 2, ROWS, 128), "space")
    middle = temporal(t, outproj_time, queryproj_time, keyproj_time, valueproj_time)
    middle, qk = lax.optimization_barrier((middle, qk))
    middle = exchange(middle, "tm")
    middle_grad, vg = project(middle, outproj_space, value_space)
    vg, qk = lax.optimization_barrier((vg, qk))
    p = probs(half, qk)
    vg = exchange(vg.reshape(16, 2, ROWS, 128), "space")
    out = exchange(grads(half, qk, vg, p), "space")
    query_grad, key_grad, value_grad = unpack(out.reshape(8, 2, 3, ROWS, 128))
    return query_grad, key_grad, value_grad, middle_grad


def solution(mesh):
    bulk = P("tm", "space", None)
    return jax.shard_map(
        per_device,
        mesh=mesh,
        in_specs=(bulk,) * 7 + (P(),) * 5,
        out_specs=(bulk,) * 4,
        check_vma=False,
    )
```
